32 devices in a mesh: row: 16 (over z, x, core), col: 2 (over y).
Axes of the slice: x: 2, y: 2, z: 4, core: 2. Of those that a mesh axis runs over, the one named last changes fastest.
Arguments:
- tokens: bfloat16 [1024, 12288], P('col', 'row'), may hold values from -6 to 6
- weight: bfloat16 [12288, 24576], P('row', 'col'), may hold values from -0.0546875 to 0.0546875
- pre_act: bfloat16 [1024, 24576], P('row', 'col'), may hold values from -6 to 6
- out_grad: bfloat16 [1024, 24576], P('row', 'col'), may hold values from -6 to 6
Outputs:
- input_grad: bfloat16 [1024, 12288], P('col', 'row')
- weight_grad: bfloat16 [12288, 24576], P('row', 'col')
- left_stats: bfloat16 [12288, 24576], P('row', 'col')
- right_stats: bfloat16 [12288, 24576], P('row', 'col')
The draws below stay inside these ranges and needn't reach their ends.
All inputs are finite; a program needn't handle non-finite values.
Results may differ from the reference program's by a relative error of at most 0.0054.
Values may be sent and summed in bfloat16 or wider, within the bound.
No kernel may reach another device: no remote copies, remote signals or barrier semaphores. Data moves between devices by JAX's collectives and lax.ppermute only.
A program may use at most 256 MiB of HBM per device.

```python
import math
import jax
import jax.numpy as jnp
from jax import lax

D = 12288
FF = 24576
BLOCK = 384
TOKENS = 1024


def level_of(own_key, shape, split, least, largest):
    level, own = 1.0, jax.random.fold_in(own_key, 6)
    for axis_at, shards_of in split:
        steps = jnp.exp(jax.random.uniform(jax.random.fold_in(own, axis_at), (shards_of,), jnp.float32, least / len(split), largest / len(split)))
        level = level * jnp.repeat(steps, shape[axis_at] // shards_of).reshape([-1 if axis == axis_at else 1 for axis in range(len(shape))])
    return level


def bell_draw(own_key, shape, scale, most, shards=(), kind=jnp.bfloat16):
    drawn = scale * jax.random.normal(own_key, shape, jnp.float32)
    if shards:
        drawn = drawn * level_of(own_key, shape, shards, -0.22, 0.18)
    return jnp.clip(drawn, -most, most).astype(kind)


def setup_inputs(seed: int = 0) -> dict:
    streams_of = jax.random.split(jax.random.key(seed), 5)
    tokens = bell_draw(streams_of[0], (TOKENS, D), 1.0, 6.0, ((0, 2), (1, 16)))
    weight = bell_draw(streams_of[1], (D, FF), D ** -0.5, 0.0546875, ((0, 16), (1, 2)))
    pre_act = bell_draw(streams_of[2], (TOKENS, FF), 1.0, 6.0, ((0, 16), (1, 2)))
    out_grad = bell_draw(streams_of[3], (TOKENS, FF), 1.0, 6.0, ((0, 16), (1, 2)))
    return {"tokens": tokens, "weight": weight, "pre_act": pre_act, "out_grad": out_grad}


def gelu_slope(value):
    coeff = math.sqrt(2.0 / math.pi)
    inner = coeff * (value + 0.044715 * value * value * value)
    tanh_u = jnp.tanh(inner)
    return 0.5 * (1.0 + tanh_u) + 0.5 * value * (1.0 - tanh_u * tanh_u) * coeff * (1.0 + 3.0 * 0.044715 * value * value)

def reference(tokens, weight, pre_act, out_grad):
    num_tokens = tokens.shape[0]
    scale = 1.0 / (BLOCK * num_tokens)

    def one_block(carry, index):
        start = index * BLOCK
        h_blk = lax.dynamic_slice_in_dim(pre_act, start, BLOCK, 1).astype(jnp.float32)
        g_blk = lax.dynamic_slice_in_dim(out_grad, start, BLOCK, 1).astype(jnp.float32)
        hidden_grad = (g_blk * gelu_slope(h_blk)).astype(jnp.bfloat16)
        w_blk = lax.dynamic_slice_in_dim(weight, start, BLOCK, 1)
        carry = carry + lax.dot_general(hidden_grad, w_blk, (((1,), (1,)), ((), ())), preferred_element_type=jnp.float32)
        weight_sum = lax.dot_general(tokens, hidden_grad, (((0,), (0,)), ((), ())), preferred_element_type=jnp.float32)
        tiles = weight_sum.reshape(D // BLOCK, BLOCK, BLOCK)
        left = jnp.einsum('ipq,irq->ipr', tiles, tiles, precision=lax.Precision.HIGHEST) * scale
        right = jnp.einsum('ipq,ipr->iqr', tiles, tiles, precision=lax.Precision.HIGHEST) * scale
        return (carry, (weight_sum.astype(jnp.bfloat16), left.reshape(D, BLOCK).astype(jnp.bfloat16), right.reshape(D, BLOCK).astype(jnp.bfloat16)))
    init = jnp.zeros((num_tokens, D), jnp.float32)
    indices = jnp.arange(FF // BLOCK, dtype=jnp.int32)
    summed, (grads, lefts, rights) = lax.scan(one_block, init, indices)

    def place(stacked):
        return jnp.transpose(stacked, (1, 0, 2)).reshape(D, FF)
    return (summed.astype(jnp.bfloat16), place(grads), place(lefts), place(rights))
```

```python
import functools
import math

import jax
import jax.numpy as jnp
from jax import lax
from jax.experimental import pallas as pl
from jax.experimental.pallas import tpu as pltpu
from jax.sharding import PartitionSpec as P

BLOCK = 384
STEP = 2 * BLOCK
SHARES = (6, 5, 3, 2)
VMEM_LIMIT = 56 * 1024 * 1024


def gelu_slope(value):
    coeff = math.sqrt(2.0 / math.pi)
    inner = coeff * (value + 0.044715 * value * value * value)
    tanh_u = jnp.tanh(inner)
    return 0.5 * (1.0 + tanh_u) + 0.5 * value * (1.0 - tanh_u * tanh_u) * coeff * (
        1.0 + 3.0 * 0.044715 * value * value
    )


def chunk_steps(steps):
    bounds, done = [0], 0
    for share in SHARES:
        done += share
        bounds.append(round(steps * done / sum(SHARES)))
    return [(a, b - a) for a, b in zip(bounds, bounds[1:]) if b > a]


def block_stats(scale, grad_f32, wg_ref, left_ref, right_ref):
    rows, cols = grad_f32.shape
    wg_ref[...] = grad_f32.astype(wg_ref.dtype)
    for i in range(rows // BLOCK):
        for j in range(cols // BLOCK):
            at = (pl.ds(i * BLOCK, BLOCK), pl.ds(j * BLOCK, BLOCK))
            tile = wg_ref[at]
            left = lax.dot_general(
                tile, tile, (((1,), (1,)), ((), ())), preferred_element_type=jnp.float32
            )
            left_ref[at] = (left * scale).astype(left_ref.dtype)
            right = lax.dot_general(
                tile, tile, (((0,), (0,)), ((), ())), preferred_element_type=jnp.float32
            )
            right_ref[at] = (right * scale).astype(right_ref.dtype)


def chunk_kernel(scale, with_share, first, *refs):
    n_in = 2 + (1 if with_share else 0) + (1 if with_share and not first else 0)
    ins, outs = refs[:n_in], refs[n_in + (0 if first else 3):]
    xt_ref, hg_ref = ins[:2]
    wg_ref, left_ref, right_ref = outs[:3]
    if with_share:
        w_ref, acc_ref = ins[2], outs[3]

        @pl.when(pl.program_id(0) == 0)
        def _():
            if first:
                acc_ref[...] = jnp.zeros_like(acc_ref)
            else:
                acc_ref[...] = ins[3][...]

        acc_ref[...] += lax.dot_general(
            hg_ref[...], w_ref[...], (((1,), (1,)), ((), ())), preferred_element_type=jnp.float32
        )
    grad = jnp.dot(xt_ref[...], hg_ref[...], preferred_element_type=jnp.float32)
    block_stats(scale, grad, wg_ref, left_ref, right_ref)


def chunk_call(scale, x_t, hg, weight, acc, outs, offset, steps, with_share):
    rows, tokens = x_t.shape
    first = outs is None
    at = lambda s: (0, s + offset)
    args = [x_t, hg]
    in_specs = [
        pl.BlockSpec((rows, tokens), lambda s: (0, 0)),
        pl.BlockSpec((tokens, STEP), lambda s: (0, s)),
    ]
    out_shape = [jax.ShapeDtypeStruct(weight.shape, jnp.bfloat16)] * 3
    out_specs = [pl.BlockSpec((rows, STEP), at)] * 3
    if with_share:
        args.append(weight)
        in_specs.append(pl.BlockSpec((rows, STEP), at))
        out_shape = out_shape + [jax.ShapeDtypeStruct((tokens, rows), jnp.float32)]
        out_specs = out_specs + [pl.BlockSpec((tokens, rows), lambda s: (0, 0))]
        if not first:
            args.append(acc)
            in_specs.append(pl.BlockSpec((tokens, rows), lambda s: (0, 0)))
    aliases = {}
    if not first:
        aliases = {len(args) + i: i for i in range(3)}
        args += list(outs)
        in_specs += [pl.BlockSpec(memory_space=pl.ANY)] * 3
    cells = steps * STEP * rows
    return pl.pallas_call(
        functools.partial(chunk_kernel, scale, with_share, first),
        grid=(steps,),
        in_specs=in_specs,
        out_specs=out_specs,
        out_shape=out_shape,
        input_output_aliases=aliases,
        compiler_params=pltpu.CompilerParams(vmem_limit_bytes=VMEM_LIMIT),
        cost_estimate=pl.CostEstimate(
            flops=cells * (2 * tokens * (2 if with_share else 1) + 4 * BLOCK),
            bytes_accessed=8 * cells + 2 * steps * STEP * tokens,
            transcendentals=0,
        ),
        name="chunk",
    )(*args)


def share_kernel(_, hg_ref, w_ref, acc_ref, out_ref):
    total = acc_ref[...] + lax.dot_general(
        hg_ref[...], w_ref[...], (((1,), (1,)), ((), ())), preferred_element_type=jnp.float32
    )
    out_ref[...] = total[None].astype(out_ref.dtype)


def share_call(which, hg, weight, acc, count, offset, dtype):
    tokens, width = hg.shape
    rows = weight.shape[0]
    group = tokens // count
    tile = 256 if rows % 256 == 0 else BLOCK
    pieces = which.shape[0]
    grid_spec = pltpu.PrefetchScalarGridSpec(
        num_scalar_prefetch=1,
        grid=(pieces, rows // tile),
        in_specs=[
            pl.BlockSpec((group, width), lambda p, d, w: (w[p], 0)),
            pl.BlockSpec((tile, width), lambda p, d, w: (d, 0)),
            pl.BlockSpec((group, tile), lambda p, d, w: (w[p], d)),
        ],
        out_specs=pl.BlockSpec((1, group, tile), lambda p, d, w: (p, 0, d)),
    )
    w_last = weight[:, offset * STEP:]
    return pl.pallas_call(
        share_kernel,
        grid_spec=grid_spec,
        out_shape=jax.ShapeDtypeStruct((pieces, group, rows), dtype),
        compiler_params=pltpu.CompilerParams(vmem_limit_bytes=VMEM_LIMIT),
        cost_estimate=pl.CostEstimate(
            flops=2 * pieces * group * width * rows,
            bytes_accessed=2 * rows * width + pieces * group * (2 * width + 6 * rows),
            transcendentals=0,
        ),
        name="share",
    )(which, hg, w_last, acc)


def on_device(cols, tokens, weight, pre_act, out_grad):
    me = lax.axis_index("col")
    group, rows = tokens.shape
    num_tokens = group * cols
    scale = 1.0 / (BLOCK * num_tokens)
    chunks = chunk_steps(weight.shape[1] // STEP)

    gathered = []
    for offset, steps in chunks:
        at = slice(offset * STEP, (offset + steps) * STEP)
        slope = gelu_slope(pre_act[:, at].astype(jnp.float32))
        hidden = (out_grad[:, at].astype(jnp.float32) * slope).astype(jnp.bfloat16)
        gathered.append(lax.all_gather(hidden, "row", axis=0, tiled=True))

    own_t = tokens.T
    x_t = jnp.zeros((rows, num_tokens), jnp.bfloat16)
    x_t = lax.dynamic_update_slice(x_t, own_t, (0, me * group))
    for s in range(1, cols):
        piece = lax.ppermute(own_t, "col", [(i, (i + s) % cols) for i in range(cols)])
        x_t = lax.dynamic_update_slice(x_t, piece, (0, (me - s) % cols * group))

    acc, outs = None, None
    for (offset, steps), hg in zip(chunks[:-1], gathered[:-1]):
        *outs, acc = chunk_call(scale, x_t, hg, weight, acc, outs, offset, steps, True)

    offset, steps = chunks[-1]
    hg = gathered[-1]
    others = (me + jnp.arange(1, cols, dtype=jnp.int32)) % cols
    shares = share_call(others, hg, weight, acc, cols, offset, jnp.bfloat16)
    arrived = [
        lax.ppermute(shares[s - 1], "col", [(i, (i + s) % cols) for i in range(cols)])
        for s in range(1, cols)
    ]
    own = share_call(me[None], hg, weight, acc, cols, offset, jnp.float32)[0]
    outs = chunk_call(scale, x_t, hg, weight, None, outs, offset, steps, False)
    for piece in arrived:
        own = own + piece.astype(jnp.float32)
    return (own.astype(jnp.bfloat16), *outs)


def solution(mesh):
    in_specs = (P("col", "row"), P("row", "col"), P("row", "col"), P("row", "col"))
    out_specs = (P("col", "row"), P("row", "col"), P("row", "col"), P("row", "col"))
    return jax.shard_map(
        functools.partial(on_device, mesh.shape["col"]),
        mesh=mesh,
        in_specs=in_specs,
        out_specs=out_specs,
        check_vma=False,
    )
```

```python
import functools
import math

import jax
import jax.numpy as jnp
import numpy as np
from jax import lax
from jax.experimental import pallas as pl
from jax.experimental.pallas import tpu as pltpu
from jax.sharding import PartitionSpec as P

BLOCK = 384
STEP = 2 * BLOCK
CHUNKS = (1, 2, 2, 2, 1)
VMEM_LIMIT = 60 * 1024 * 1024
ANYWHERE = pl.BlockSpec(memory_space=pltpu.HBM)
TICK = jax.ShapeDtypeStruct((8, 128), jnp.float32)
NT = (((1,), (1,)), ((), ()))
TN = (((0,), (0,)), ((), ()))


def gelu_slope(value):
    coeff = math.sqrt(2.0 / math.pi)
    inner = coeff * (value + 0.044715 * value * value * value)
    tanh_u = jnp.tanh(inner)
    return 0.5 * (1.0 + tanh_u) + 0.5 * value * (1.0 - tanh_u * tanh_u) * coeff * (
        1.0 + 3.0 * 0.044715 * value * value
    )


def plan(steps):
    pairs, total = steps // 2, sum(CHUNKS)
    bounds, done = [0], 0
    for share in CHUNKS:
        done += share
        bounds.append(round(pairs * done / total))
    return [(2 * a, 2 * (b - a)) for a, b in zip(bounds, bounds[1:]) if b > a]


def gate_kernel(*refs):
    del refs


def gate_call(pieces, ticks):
    count = len(pieces)
    result = pl.pallas_call(
        gate_kernel,
        in_specs=[ANYWHERE] * (count + len(ticks)),
        out_specs=[ANYWHERE] * (count + 1),
        out_shape=[jax.ShapeDtypeStruct(p.shape, p.dtype) for p in pieces] + [TICK],
        input_output_aliases={i: i for i in range(count)},
        name="gate",
    )(*pieces, *ticks)
    return result[:count], result[count]


def merge_kernel(count, place_ref, *refs):
    pieces, (out_ref, sems) = refs[:count], refs[-2:]
    copies = []
    for k, piece in enumerate(pieces):
        rows = piece.shape[0]
        at = pl.multiple_of(place_ref[k], rows)
        copies.append(pltpu.make_async_copy(piece, out_ref.at[pl.ds(at, rows), :], sems.at[k]))
        copies[-1].start()
    for copy in copies:
        copy.wait()


def merge_call(places, pieces, ticks):
    count = len(pieces)
    tokens = sum(piece.shape[0] for piece in pieces)
    width = pieces[0].shape[1]
    return pl.pallas_call(
        functools.partial(merge_kernel, count),
        grid_spec=pltpu.PrefetchScalarGridSpec(
            num_scalar_prefetch=1,
            grid=(1,),
            in_specs=[ANYWHERE] * (count + len(ticks)),
            out_specs=ANYWHERE,
            scratch_shapes=[pltpu.SemaphoreType.DMA((count,))],
        ),
        out_shape=jax.ShapeDtypeStruct((tokens, width), pieces[0].dtype),
        cost_estimate=pl.CostEstimate(
            flops=0, bytes_accessed=4 * tokens * width, transcendentals=0
        ),
        name="merge",
    )(places, *pieces, *ticks)


def chunk_kernel(scale, halves, half_steps, with_share, first, n_ticks, off_ref, *refs):
    refs = list(refs)
    xt_ref = refs.pop(0)
    hg_refs = [refs.pop(0) for _ in range(halves)]
    w_ref = refs.pop(0) if with_share else None
    acc_in = refs.pop(0) if with_share and not first else None
    del refs[:n_ticks]
    if not first:
        del refs[:3]
    wg_ref, left_ref, right_ref, tick_ref = refs[:4]
    refs = refs[4:]
    step, steps = pl.program_id(0), halves * half_steps
    if with_share:
        acc_out, acc_ref, in_sem, out_sem = refs

    @pl.when(step == 0)
    def _():
        tick_ref[...] = jnp.zeros_like(tick_ref)
        if with_share:
            if first:
                acc_ref[...] = jnp.zeros_like(acc_ref)
            else:
                pltpu.make_async_copy(acc_in, acc_ref, in_sem).start()

    def work(hg_ref):
        grad = jnp.dot(xt_ref[...], hg_ref[...], preferred_element_type=jnp.float32)
        wg_ref[...] = grad.astype(wg_ref.dtype)

        if with_share:
            if not first:

                @pl.when(step == 0)
                def _():
                    pltpu.make_async_copy(acc_in, acc_ref, in_sem).wait()

            acc_ref[...] += lax.dot_general(
                hg_ref[...], w_ref[...], NT, preferred_element_type=jnp.float32
            )

            @pl.when(step == steps - 1)
            def _():
                pltpu.make_async_copy(acc_ref, acc_out, out_sem).start()

    if halves == 1:
        work(hg_refs[0])
    else:
        for k in range(halves):
            pl.when(step // half_steps == k)(functools.partial(work, hg_refs[k]))

    rows, cols = wg_ref.shape
    for i in range(rows // BLOCK):
        for j in range(cols // BLOCK):
            at = (pl.ds(i * BLOCK, BLOCK), pl.ds(j * BLOCK, BLOCK))
            tile = wg_ref[at]
            left = lax.dot_general(tile, tile, NT, preferred_element_type=jnp.float32)
            left_ref[at] = (left * scale).astype(left_ref.dtype)
            right = lax.dot_general(tile, tile, TN, preferred_element_type=jnp.float32)
            right_ref[at] = (right * scale).astype(right_ref.dtype)

    if with_share:

        @pl.when(step == steps - 1)
        def _():
            pltpu.make_async_copy(acc_ref, acc_out, out_sem).wait()


def chunk_call(scale, offs, x_t, hgs, weight, acc, outs, ticks, with_share):
    rows, tokens = x_t.shape
    halves, half_steps = len(hgs), hgs[0].shape[1] // STEP
    first = outs is None

    def at(s, off):
        return (0, off[s // half_steps] + s % half_steps)

    def part(k):
        return lambda s, off: (0, jnp.clip(s - k * half_steps, 0, half_steps - 1))

    args = [x_t] + hgs
    in_specs = [pl.BlockSpec((rows, tokens), lambda s, off: (0, 0))]
    in_specs += [pl.BlockSpec((tokens, STEP), part(k)) for k in range(halves)]
    out_shape = [jax.ShapeDtypeStruct(weight.shape, jnp.bfloat16)] * 3 + [TICK]
    out_specs = [pl.BlockSpec((rows, STEP), at)] * 3
    out_specs.append(pl.BlockSpec(TICK.shape, lambda s, off: (0, 0)))
    scratch = []
    aliases = {}
    if with_share:
        args.append(weight)
        in_specs.append(pl.BlockSpec((rows, STEP), at))
        out_shape.append(jax.ShapeDtypeStruct((tokens, rows), jnp.float32))
        out_specs.append(ANYWHERE)
        scratch += [
            pltpu.VMEM((tokens, rows), jnp.float32),
            pltpu.SemaphoreType.DMA,
            pltpu.SemaphoreType.DMA,
        ]
        if not first:
            args.append(acc)
            in_specs.append(ANYWHERE)
    args += ticks
    in_specs += [ANYWHERE] * len(ticks)
    if not first:
        aliases = {1 + len(args) + i: i for i in range(3)}
        args += list(outs)
        in_specs += [ANYWHERE] * 3
    cells = halves * half_steps * STEP * rows
    return pl.pallas_call(
        functools.partial(
            chunk_kernel, scale, halves, half_steps, with_share, first, len(ticks)
        ),
        grid_spec=pltpu.PrefetchScalarGridSpec(
            num_scalar_prefetch=1,
            grid=(halves * half_steps,),
            in_specs=in_specs,
            out_specs=out_specs,
            scratch_shapes=scratch,
        ),
        out_shape=out_shape,
        input_output_aliases=aliases,
        compiler_params=pltpu.CompilerParams(vmem_limit_bytes=VMEM_LIMIT),
        cost_estimate=pl.CostEstimate(
            flops=cells * (2 * tokens * (2 if with_share else 1) + 4 * BLOCK),
            bytes_accessed=8 * cells + 2 * halves * half_steps * STEP * tokens,
            transcendentals=0,
        ),
        name="chunk",
    )(offs, *args)


def share_kernel(groups, group, half_steps, who_ref, off_ref, *refs):
    own_hg, other_hg, w_ref, acc_ref, away_ref, own_ref, sum_ref = refs
    step = pl.program_id(0)

    @pl.when(step == 0)
    def _():
        sum_ref[...] = acc_ref[...]

    for k, hg_ref in enumerate((own_hg, other_hg)):

        @pl.when(step // half_steps == k)
        def _(hg_ref=hg_ref):
            sum_ref[...] += lax.dot_general(
                hg_ref[...], w_ref[...], NT, preferred_element_type=jnp.float32
            )

    @pl.when(step == 2 * half_steps - 1)
    def _():
        for k in range(groups):
            at = pl.multiple_of(who_ref[k] * group, group)
            part = sum_ref[pl.ds(at, group), :]
            if k:
                away_ref[k - 1] = part.astype(away_ref.dtype)
            else:
                own_ref[...] = part


def share_call(who, offs, hgs, weight, acc, groups):
    tokens, rows = acc.shape
    group = tokens // groups
    half_steps = hgs[0].shape[1] // STEP

    def part(k):
        return lambda s, who, off: (0, jnp.clip(s - k * half_steps, 0, half_steps - 1))

    return pl.pallas_call(
        functools.partial(share_kernel, groups, group, half_steps),
        grid_spec=pltpu.PrefetchScalarGridSpec(
            num_scalar_prefetch=2,
            grid=(2 * half_steps,),
            in_specs=[
                pl.BlockSpec((tokens, STEP), part(0)),
                pl.BlockSpec((tokens, STEP), part(1)),
                pl.BlockSpec(
                    (rows, STEP),
                    lambda s, who, off: (0, off[s // half_steps] + s % half_steps),
                ),
                pl.BlockSpec((tokens, rows), lambda s, *_: (0, 0)),
            ],
            out_specs=[
                pl.BlockSpec((groups - 1, group, rows), lambda s, *_: (0, 0, 0)),
                pl.BlockSpec((group, rows), lambda s, *_: (0, 0)),
            ],
            scratch_shapes=[pltpu.VMEM((tokens, rows), jnp.float32)],
        ),
        out_shape=[
            jax.ShapeDtypeStruct((groups - 1, group, rows), jnp.bfloat16),
            jax.ShapeDtypeStruct((group, rows), jnp.float32),
        ],
        compiler_params=pltpu.CompilerParams(vmem_limit_bytes=VMEM_LIMIT),
        cost_estimate=pl.CostEstimate(
            flops=4 * tokens * half_steps * STEP * rows,
            bytes_accessed=4 * half_steps * STEP * (rows + tokens) + 8 * tokens * rows,
            transcendentals=0,
        ),
        name="share",
    )(who, offs, *hgs, weight, acc)


class Ring:
    def __init__(self, size):
        self.chips = size // 2
        self.order = list(range(0, self.chips, 2)) + list(range(1, self.chips, 2))[::-1]
        self.hops = self.chips // 2

    def shift(self, value, by):
        pairs = []
        for k, chip in enumerate(self.order):
            to = self.order[(k + by) % self.chips]
            pairs += [(2 * chip + core, 2 * to + core) for core in range(2)]
        return lax.ppermute(value, "row", pairs)

    def swap(self, value):
        return lax.ppermute(value, "row", [(i, i ^ 1) for i in range(2 * self.chips)])

    def places(self, rows_each):
        table = []
        for row in range(2 * self.chips):
            pos = self.order.index(row // 2)
            base = lambda by: self.order[(pos + by) % self.chips] * rows_each
            line = [base(0)]
            for hop in range(1, self.hops):
                line += [base(-hop), base(hop)]
            line += [base(-self.hops), base(self.hops) + rows_each // 2]
            table.append(line)
        return jnp.asarray(np.array(table, np.int32))[lax.axis_index("row")]


class Stream:
    def __init__(self, ring, piece):
        self.ring, self.fresh, self.kept, self.hop = ring, [piece], [], 0

    def advance(self):
        ring = self.ring
        self.kept += self.fresh
        ahead, behind = (self.fresh * 2)[:2]
        self.hop += 1
        if self.hop == ring.hops:
            half = ahead.shape[0] // 2
            ahead, behind = ahead[:half], behind[half:]
        self.fresh = [ring.shift(ahead, 1), ring.shift(behind, -1)]

    def gate(self, ticks):
        self.fresh, tick = gate_call(self.fresh, ticks)
        return tick

    def pieces(self):
        return self.kept + self.fresh


def on_device(row_size, cols, tokens, weight, pre_act, out_grad):
    me, core = lax.axis_index("col"), lax.axis_index("row") % 2
    group, rows = tokens.shape
    num_tokens = group * cols
    scale = 1.0 / (BLOCK * num_tokens)
    chunks = plan(weight.shape[1] // STEP)
    ring = Ring(row_size)
    places = ring.places(2 * pre_act.shape[0])

    def hidden_of(start, width):
        h = lax.dynamic_slice_in_dim(pre_act, start, width, 1).astype(jnp.float32)
        g = lax.dynamic_slice_in_dim(out_grad, start, width, 1).astype(jnp.float32)
        return (g * gelu_slope(h)).astype(jnp.bfloat16)

    def stream_of(chunk):
        first, half = chunk[0] * STEP, chunk[1] * STEP // 2
        got = ring.swap(hidden_of(first + (1 - core) * half, half))
        mine = hidden_of(first + core * half, half)
        upper, lower = jnp.where(core == 0, mine, got), jnp.where(core == 0, got, mine)
        return Stream(ring, jnp.concatenate([upper, lower], axis=0))

    streams = [stream_of(chunk) for chunk in chunks]
    offsets = [
        jnp.stack([a + core * (n // 2), a + (1 - core) * (n // 2)]).astype(jnp.int32)
        for a, n in chunks
    ]

    own_t = tokens.T
    x_t = jnp.zeros((rows, num_tokens), jnp.bfloat16)
    x_t = lax.dynamic_update_slice(x_t, own_t, (0, me * group))
    for s in range(1, cols):
        piece = lax.ppermute(own_t, "col", [(i, (i + s) % cols) for i in range(cols)])
        x_t = lax.dynamic_update_slice(x_t, piece, (0, (me - s) % cols * group))

    def advance(k, upto, ticks):
        out = []
        if k < len(streams):
            while streams[k].hop < upto:
                if ticks:
                    out = [streams[k].gate(ticks)]
                streams[k].advance()
        return out

    half, last = ring.hops // 2, len(chunks) - 1
    advance(0, half, [])
    if last:
        advance(0, half + 1, [streams[1].fresh[0]])
    advance(1, half, [])
    advance(0, ring.hops, [])
    acc, outs, ticks = None, None, []
    for k in range(len(chunks)):
        seen = advance(k + 1, half + 1, ticks) + advance(k + 2, 1, ticks)
        own = merge_call(places, streams[k].pieces(), seen)
        other = ring.swap(own)
        offs = offsets[k]
        if k < last:
            *outs, tick, acc = chunk_call(
                scale, offs[:1], x_t, [own], weight, acc, outs, seen, True
            )
            seen = advance(k + 1, ring.hops, [tick]) + advance(k + 2, half, [tick])
            *outs, tick, acc = chunk_call(
                scale, offs[1:], x_t, [other], weight, acc, outs, seen, True
            )
            ticks = [tick]
    who = (me + jnp.arange(cols, dtype=jnp.int32)) % cols
    away, share = share_call(who, offs, [own, other], weight, acc, cols)
    arrived = [
        lax.ppermute(away[s - 1], "col", [(i, (i + s) % cols) for i in range(cols)])
        for s in range(1, cols)
    ]
    *outs, tick = chunk_call(
        scale, offs, x_t, [own, other], weight, None, outs, [share], False
    )
    for piece in arrived:
        share = share + piece.astype(jnp.float32)
    return (share.astype(jnp.bfloat16), *outs)


def solution(mesh):
    in_specs = (P("col", "row"), P("row", "col"), P("row", "col"), P("row", "col"))
    out_specs = (P("col", "row"), P("row", "col"), P("row", "col"), P("row", "col"))
    return jax.shard_map(
        functools.partial(on_device, mesh.shape["row"], mesh.shape["col"]),
        mesh=mesh,
        in_specs=in_specs,
        out_specs=out_specs,
        check_vma=False,
    )
```

```python
import functools
import math

import jax
import jax.numpy as jnp
from jax import lax
from jax.experimental import pallas as pl
from jax.experimental.pallas import tpu as pltpu
from jax.sharding import PartitionSpec as P

BLOCK = 384
STEP = 2 * BLOCK
SHARES = (1, 1)
VMEM_LIMIT = 56 * 1024 * 1024


def gelu_slope(value):
    coeff = math.sqrt(2.0 / math.pi)
    inner = coeff * (value + 0.044715 * value * value * value)
    tanh_u = jnp.tanh(inner)
    return 0.5 * (1.0 + tanh_u) + 0.5 * value * (1.0 - tanh_u * tanh_u) * coeff * (
        1.0 + 3.0 * 0.044715 * value * value
    )


def chunk_steps(steps):
    bounds, done = [0], 0
    for share in SHARES:
        done += share
        bounds.append(round(steps * done / sum(SHARES)))
    return [(a, b - a) for a, b in zip(bounds, bounds[1:]) if b > a]


def block_stats(scale, grad_f32, wg_ref, left_ref, right_ref):
    rows, cols = grad_f32.shape
    wg_ref[...] = grad_f32.astype(wg_ref.dtype)
    for i in range(rows // BLOCK):
        for j in range(cols // BLOCK):
            at = (pl.ds(i * BLOCK, BLOCK), pl.ds(j * BLOCK, BLOCK))
            tile = wg_ref[at]
            left = lax.dot_general(
                tile, tile, (((1,), (1,)), ((), ())), preferred_element_type=jnp.float32
            )
            left_ref[at] = (left * scale).astype(left_ref.dtype)
            right = lax.dot_general(
                tile, tile, (((0,), (0,)), ((), ())), preferred_element_type=jnp.float32
            )
            right_ref[at] = (right * scale).astype(right_ref.dtype)


def chunk_kernel(scale, with_share, first, *refs):
    n_in = 2 + (1 if with_share else 0) + (1 if with_share and not first else 0)
    ins, outs = refs[:n_in], refs[n_in + (0 if first else 3):]
    xt_ref, hg_ref = ins[:2]
    wg_ref, left_ref, right_ref = outs[:3]
    if with_share:
        w_ref, acc_ref = ins[2], outs[3]

        @pl.when(pl.program_id(0) == 0)
        def _():
            if first:
                acc_ref[...] = jnp.zeros_like(acc_ref)
            else:
                acc_ref[...] = ins[3][...]

        acc_ref[...] += lax.dot_general(
            hg_ref[...], w_ref[...], (((1,), (1,)), ((), ())), preferred_element_type=jnp.float32
        )
    grad = jnp.dot(xt_ref[...], hg_ref[...], preferred_element_type=jnp.float32)
    block_stats(scale, grad, wg_ref, left_ref, right_ref)


def chunk_call(scale, x_t, hg, weight, acc, outs, offset, steps, with_share):
    rows, tokens = x_t.shape
    first = outs is None
    at = lambda s: (0, s + offset)
    args = [x_t, hg]
    in_specs = [
        pl.BlockSpec((rows, tokens), lambda s: (0, 0)),
        pl.BlockSpec((tokens, STEP), lambda s: (0, s)),
    ]
    out_shape = [jax.ShapeDtypeStruct(weight.shape, jnp.bfloat16)] * 3
    out_specs = [pl.BlockSpec((rows, STEP), at)] * 3
    if with_share:
        args.append(weight)
        in_specs.append(pl.BlockSpec((rows, STEP), at))
        out_shape = out_shape + [jax.ShapeDtypeStruct((tokens, rows), jnp.float32)]
        out_specs = out_specs + [pl.BlockSpec((tokens, rows), lambda s: (0, 0))]
        if not first:
            args.append(acc)
            in_specs.append(pl.BlockSpec((tokens, rows), lambda s: (0, 0)))
    aliases = {}
    if not first:
        aliases = {len(args) + i: i for i in range(3)}
        args += list(outs)
        in_specs += [pl.BlockSpec(memory_space=pl.ANY)] * 3
    cells = steps * STEP * rows
    return pl.pallas_call(
        functools.partial(chunk_kernel, scale, with_share, first),
        grid=(steps,),
        in_specs=in_specs,
        out_specs=out_specs,
        out_shape=out_shape,
        input_output_aliases=aliases,
        compiler_params=pltpu.CompilerParams(vmem_limit_bytes=VMEM_LIMIT),
        cost_estimate=pl.CostEstimate(
            flops=cells * (2 * tokens * (2 if with_share else 1) + 4 * BLOCK),
            bytes_accessed=8 * cells + 2 * steps * STEP * tokens,
            transcendentals=0,
        ),
        name="chunk",
    )(*args)


def share_kernel(groups, group, steps, who_ref, hg_ref, w_ref, acc_ref, away_ref, own_ref, sum_ref):
    step = pl.program_id(0)

    @pl.when(step == 0)
    def _():
        sum_ref[...] = acc_ref[...]

    sum_ref[...] += lax.dot_general(
        hg_ref[...], w_ref[...], (((1,), (1,)), ((), ())), preferred_element_type=jnp.float32
    )

    @pl.when(step == steps - 1)
    def _():
        for k in range(groups):
            at = pl.multiple_of(who_ref[k] * group, group)
            part = sum_ref[pl.ds(at, group), :]
            if k:
                away_ref[k - 1] = part.astype(away_ref.dtype)
            else:
                own_ref[...] = part


def share_call(who, hg, weight, acc, groups, offset, steps):
    tokens, rows = acc.shape
    group = tokens // groups
    return pl.pallas_call(
        functools.partial(share_kernel, groups, group, steps),
        grid_spec=pltpu.PrefetchScalarGridSpec(
            num_scalar_prefetch=1,
            grid=(steps,),
            in_specs=[
                pl.BlockSpec((tokens, STEP), lambda s, _: (0, s)),
                pl.BlockSpec((rows, STEP), lambda s, _: (0, s + offset)),
                pl.BlockSpec((tokens, rows), lambda s, _: (0, 0)),
            ],
            out_specs=[
                pl.BlockSpec((groups - 1, group, rows), lambda s, _: (0, 0, 0)),
                pl.BlockSpec((group, rows), lambda s, _: (0, 0)),
            ],
            scratch_shapes=[pltpu.VMEM((tokens, rows), jnp.float32)],
        ),
        out_shape=[
            jax.ShapeDtypeStruct((groups - 1, group, rows), jnp.bfloat16),
            jax.ShapeDtypeStruct((group, rows), jnp.float32),
        ],
        compiler_params=pltpu.CompilerParams(vmem_limit_bytes=VMEM_LIMIT),
        cost_estimate=pl.CostEstimate(
            flops=2 * tokens * steps * STEP * rows,
            bytes_accessed=2 * steps * STEP * (rows + tokens) + 8 * tokens * rows,
            transcendentals=0,
        ),
        name="share",
    )(who, hg, weight, acc)


def on_device(cols, tokens, weight, pre_act, out_grad):
    me = lax.axis_index("col")
    group, rows = tokens.shape
    num_tokens = group * cols
    scale = 1.0 / (BLOCK * num_tokens)
    chunks = chunk_steps(weight.shape[1] // STEP)

    gathered = []
    for offset, steps in chunks:
        at = slice(offset * STEP, (offset + steps) * STEP)
        slope = gelu_slope(pre_act[:, at].astype(jnp.float32))
        hidden = (out_grad[:, at].astype(jnp.float32) * slope).astype(jnp.bfloat16)
        gathered.append(lax.all_gather(hidden, "row", axis=0, tiled=True))

    own_t = tokens.T
    x_t = jnp.zeros((rows, num_tokens), jnp.bfloat16)
    x_t = lax.dynamic_update_slice(x_t, own_t, (0, me * group))
    for s in range(1, cols):
        piece = lax.ppermute(own_t, "col", [(i, (i + s) % cols) for i in range(cols)])
        x_t = lax.dynamic_update_slice(x_t, piece, (0, (me - s) % cols * group))

    acc, outs = None, None
    for (offset, steps), hg in zip(chunks[:-1], gathered[:-1]):
        *outs, acc = chunk_call(scale, x_t, hg, weight, acc, outs, offset, steps, True)

    offset, steps = chunks[-1]
    hg = gathered[-1]
    who = (me + jnp.arange(cols, dtype=jnp.int32)) % cols
    shares, own = share_call(who, hg, weight, acc, cols, offset, steps)
    arrived = [
        lax.ppermute(shares[s - 1], "col", [(i, (i + s) % cols) for i in range(cols)])
        for s in range(1, cols)
    ]
    outs = chunk_call(scale, x_t, hg, weight, None, outs, offset, steps, False)
    for piece in arrived:
        own = own + piece.astype(jnp.float32)
    return (own.astype(jnp.bfloat16), *outs)


def solution(mesh):
    in_specs = (P("col", "row"), P("row", "col"), P("row", "col"), P("row", "col"))
    out_specs = (P("col", "row"), P("row", "col"), P("row", "col"), P("row", "col"))
    return jax.shard_map(
        functools.partial(on_device, mesh.shape["col"]),
        mesh=mesh,
        in_specs=in_specs,
        out_specs=out_specs,
        check_vma=False,
    )
```

```python
import functools
import math

import jax
import jax.numpy as jnp
import numpy as np
from jax import lax
from jax.experimental import pallas as pl
from jax.experimental.pallas import tpu as pltpu
from jax.sharding import PartitionSpec as P

BLOCK = 384
STEP = 2 * BLOCK
RING, GATHER = 0, 1
CHUNKS = ((RING, 2), (GATHER, 3), (RING, 3))
VMEM_LIMIT = 60 * 1024 * 1024
ANYWHERE = pl.BlockSpec(memory_space=pltpu.HBM)
TICK = jax.ShapeDtypeStruct((8, 128), jnp.float32)


def gelu_slope(value):
    coeff = math.sqrt(2.0 / math.pi)
    inner = coeff * (value + 0.044715 * value * value * value)
    tanh_u = jnp.tanh(inner)
    return 0.5 * (1.0 + tanh_u) + 0.5 * value * (1.0 - tanh_u * tanh_u) * coeff * (
        1.0 + 3.0 * 0.044715 * value * value
    )


def plan(steps):
    pairs, total = steps // 2, sum(share for _, share in CHUNKS)
    out, done, at = [], 0, 0
    for kind, share in CHUNKS:
        done += share
        to = round(pairs * done / total)
        if to > at:
            out.append((kind, 2 * at, 2 * (to - at)))
        at = to
    return out


def gate_kernel(*refs):
    del refs


def gate_call(pieces, ticks):
    count = len(pieces)
    result = pl.pallas_call(
        gate_kernel,
        in_specs=[ANYWHERE] * (count + len(ticks)),
        out_specs=[ANYWHERE] * (count + 1),
        out_shape=[jax.ShapeDtypeStruct(p.shape, p.dtype) for p in pieces] + [TICK],
        input_output_aliases={i: i for i in range(count)},
        name="gate",
    )(*pieces, *ticks)
    return result[:count], result[count]


def merge_kernel(place_ref, *refs):
    for k, piece in enumerate(refs[:-1]):
        rows = piece.shape[0]
        at = pl.multiple_of(place_ref[k], rows)
        refs[-1][pl.ds(at, rows), :] = piece[...]


def merge_call(places, pieces):
    tokens = sum(piece.shape[0] for piece in pieces)
    width = pieces[0].shape[1]
    return pl.pallas_call(
        merge_kernel,
        grid_spec=pltpu.PrefetchScalarGridSpec(
            num_scalar_prefetch=1,
            grid=(width // STEP,),
            in_specs=[pl.BlockSpec((p.shape[0], STEP), lambda s, _: (0, s)) for p in pieces],
            out_specs=pl.BlockSpec((tokens, STEP), lambda s, _: (0, s)),
        ),
        out_shape=jax.ShapeDtypeStruct((tokens, width), pieces[0].dtype),
        compiler_params=pltpu.CompilerParams(vmem_limit_bytes=VMEM_LIMIT),
        cost_estimate=pl.CostEstimate(
            flops=0, bytes_accessed=4 * tokens * width, transcendentals=0
        ),
        name="merge",
    )(places, *pieces)


def chunk_kernel(scale, halves, half_steps, with_share, first, n_ticks, off_ref, *refs):
    refs = list(refs)
    xt_ref = refs.pop(0)
    hg_refs = [refs.pop(0) for _ in range(halves)]
    w_ref = refs.pop(0) if with_share else None
    acc_in = refs.pop(0) if with_share and not first else None
    del refs[:n_ticks]
    if not first:
        del refs[:3]
    wg_ref, left_ref, right_ref, tick_ref = refs[:4]
    refs = refs[4:]
    step, steps = pl.program_id(0), halves * half_steps
    if with_share:
        acc_out, acc_ref, in_sem, out_sem = refs

    @pl.when(step == 0)
    def _():
        tick_ref[...] = jnp.zeros_like(tick_ref)
        if with_share:
            if first:
                acc_ref[...] = jnp.zeros_like(acc_ref)
            else:
                pltpu.make_async_copy(acc_in, acc_ref, in_sem).start()

    def work(hg_ref):
        grad = jnp.dot(xt_ref[...], hg_ref[...], preferred_element_type=jnp.float32)
        wg_ref[...] = grad.astype(wg_ref.dtype)

        if with_share:
            if not first:

                @pl.when(step == 0)
                def _():
                    pltpu.make_async_copy(acc_in, acc_ref, in_sem).wait()

            acc_ref[...] += jnp.dot(hg_ref[...], w_ref[...], preferred_element_type=jnp.float32)

            @pl.when(step == steps - 1)
            def _():
                pltpu.make_async_copy(acc_ref, acc_out, out_sem).start()

    if halves == 1:
        work(hg_refs[0])
    else:
        for k in range(halves):
            pl.when(step // half_steps == k)(functools.partial(work, hg_refs[k]))

    rows, cols = wg_ref.shape
    for i in range(rows // BLOCK):
        for j in range(cols // BLOCK):
            at = (pl.ds(i * BLOCK, BLOCK), pl.ds(j * BLOCK, BLOCK))
            tile = wg_ref[at]
            flipped = tile.T
            left = jnp.dot(tile, flipped, preferred_element_type=jnp.float32)
            left_ref[at] = (left * scale).astype(left_ref.dtype)
            right = jnp.dot(flipped, tile, preferred_element_type=jnp.float32)
            right_ref[at] = (right * scale).astype(right_ref.dtype)

    if with_share:

        @pl.when(step == steps - 1)
        def _():
            pltpu.make_async_copy(acc_ref, acc_out, out_sem).wait()


def chunk_call(scale, offs, x_t, hgs, weight_t, acc, outs, ticks, with_share):
    rows, tokens = x_t.shape
    columns = weight_t.shape[0]
    halves, half_steps = len(hgs), hgs[0].shape[1] // STEP
    first = outs is None

    def at(s, off):
        return (0, off[s // half_steps] + s % half_steps)

    def part(k):
        return lambda s, off: (0, jnp.clip(s - k * half_steps, 0, half_steps - 1))

    args = [x_t] + hgs
    in_specs = [pl.BlockSpec((rows, tokens), lambda s, off: (0, 0))]
    in_specs += [pl.BlockSpec((tokens, STEP), part(k)) for k in range(halves)]
    out_shape = [jax.ShapeDtypeStruct((rows, columns), jnp.bfloat16)] * 3 + [TICK]
    out_specs = [pl.BlockSpec((rows, STEP), at)] * 3
    out_specs.append(pl.BlockSpec(TICK.shape, lambda s, off: (0, 0)))
    scratch = []
    aliases = {}
    if with_share:
        args.append(weight_t)
        in_specs.append(pl.BlockSpec((STEP, rows), lambda s, off: at(s, off)[::-1]))
        out_shape.append(jax.ShapeDtypeStruct((tokens, rows), jnp.float32))
        out_specs.append(ANYWHERE)
        scratch += [
            pltpu.VMEM((tokens, rows), jnp.float32),
            pltpu.SemaphoreType.DMA,
            pltpu.SemaphoreType.DMA,
        ]
        if not first:
            args.append(acc)
            in_specs.append(ANYWHERE)
    args += ticks
    in_specs += [ANYWHERE] * len(ticks)
    if not first:
        aliases = {1 + len(args) + i: i for i in range(3)}
        args += list(outs)
        in_specs += [ANYWHERE] * 3
    cells = halves * half_steps * STEP * rows
    return pl.pallas_call(
        functools.partial(
            chunk_kernel, scale, halves, half_steps, with_share, first, len(ticks)
        ),
        grid_spec=pltpu.PrefetchScalarGridSpec(
            num_scalar_prefetch=1,
            grid=(halves * half_steps,),
            in_specs=in_specs,
            out_specs=out_specs,
            scratch_shapes=scratch,
        ),
        out_shape=out_shape,
        input_output_aliases=aliases,
        compiler_params=pltpu.CompilerParams(vmem_limit_bytes=VMEM_LIMIT),
        cost_estimate=pl.CostEstimate(
            flops=cells * (2 * tokens * (2 if with_share else 1) + 4 * BLOCK),
            bytes_accessed=8 * cells + 2 * halves * half_steps * STEP * tokens,
            transcendentals=0,
        ),
        name="chunk",
    )(offs, *args)


def share_kernel(groups, group, halves, half_steps, who_ref, off_ref, *refs):
    w_ref, acc_ref, away_ref, own_ref, sum_ref = refs[halves:]
    step = pl.program_id(0)

    @pl.when(step == 0)
    def _():
        sum_ref[...] = acc_ref[...]

    for k in range(halves):

        @pl.when(step // half_steps == k)
        def _(hg_ref=refs[k]):
            sum_ref[...] += jnp.dot(hg_ref[...], w_ref[...], preferred_element_type=jnp.float32)

    @pl.when(step == halves * half_steps - 1)
    def _():
        for k in range(groups):
            at = pl.multiple_of(who_ref[k] * group, group)
            part = sum_ref[pl.ds(at, group), :]
            if k:
                away_ref[k - 1] = part.astype(away_ref.dtype)
            else:
                own_ref[...] = part


def share_call(who, offs, hgs, weight_t, acc, groups):
    tokens, rows = acc.shape
    group = tokens // groups
    halves, half_steps = len(hgs), hgs[0].shape[1] // STEP
    steps = halves * half_steps

    def part(k):
        return lambda s, who, off: (0, jnp.clip(s - k * half_steps, 0, half_steps - 1))

    return pl.pallas_call(
        functools.partial(share_kernel, groups, group, halves, half_steps),
        grid_spec=pltpu.PrefetchScalarGridSpec(
            num_scalar_prefetch=2,
            grid=(steps,),
            in_specs=[pl.BlockSpec((tokens, STEP), part(k)) for k in range(halves)]
            + [
                pl.BlockSpec(
                    (STEP, rows),
                    lambda s, who, off: (off[s // half_steps] + s % half_steps, 0),
                ),
                pl.BlockSpec((tokens, rows), lambda s, *_: (0, 0)),
            ],
            out_specs=[
                pl.BlockSpec((groups - 1, group, rows), lambda s, *_: (0, 0, 0)),
                pl.BlockSpec((group, rows), lambda s, *_: (0, 0)),
            ],
            scratch_shapes=[pltpu.VMEM((tokens, rows), jnp.float32)],
        ),
        out_shape=[
            jax.ShapeDtypeStruct((groups - 1, group, rows), jnp.bfloat16),
            jax.ShapeDtypeStruct((group, rows), jnp.float32),
        ],
        compiler_params=pltpu.CompilerParams(vmem_limit_bytes=VMEM_LIMIT),
        cost_estimate=pl.CostEstimate(
            flops=2 * tokens * steps * STEP * rows,
            bytes_accessed=2 * steps * STEP * (rows + tokens) + 8 * tokens * rows,
            transcendentals=0,
        ),
        name="share",
    )(who, offs, *hgs, weight_t, acc)


class Ring:
    def __init__(self, size):
        self.chips = size // 2
        self.order = list(range(0, self.chips, 2)) + list(range(1, self.chips, 2))[::-1]
        self.hops = self.chips // 2

    def shift(self, value, by):
        pairs = []
        for k, chip in enumerate(self.order):
            to = self.order[(k + by) % self.chips]
            pairs += [(2 * chip + core, 2 * to + core) for core in range(2)]
        return lax.ppermute(value, "row", pairs)

    def swap(self, value):
        return lax.ppermute(value, "row", [(i, i ^ 1) for i in range(2 * self.chips)])

    def places(self, rows_each):
        table = []
        for row in range(2 * self.chips):
            pos = self.order.index(row // 2)
            base = lambda by: self.order[(pos + by) % self.chips] * rows_each
            line = [base(0)]
            for hop in range(1, self.hops):
                line += [base(-hop), base(hop)]
            line += [base(-self.hops), base(self.hops) + rows_each // 2]
            table.append(line)
        return jnp.asarray(np.array(table, np.int32))[lax.axis_index("row")]


class Stream:
    def __init__(self, ring, piece):
        self.ring, self.fresh, self.kept, self.hop = ring, [piece], [], 0

    def advance(self):
        ring = self.ring
        self.kept += self.fresh
        ahead, behind = (self.fresh * 2)[:2]
        self.hop += 1
        if self.hop == ring.hops:
            half = ahead.shape[0] // 2
            ahead, behind = ahead[:half], behind[half:]
        self.fresh = [ring.shift(ahead, 1), ring.shift(behind, -1)]

    def gate(self, ticks):
        self.fresh, tick = gate_call(self.fresh, ticks)
        return tick

    def pieces(self):
        return self.kept + self.fresh


def on_device(row_size, cols, tokens, weight, pre_act, out_grad):
    me, core = lax.axis_index("col"), lax.axis_index("row") % 2
    group, rows = tokens.shape
    num_tokens = group * cols
    scale = 1.0 / (BLOCK * num_tokens)
    chunks = plan(weight.shape[1] // STEP)
    ring = Ring(row_size)
    places = ring.places(2 * pre_act.shape[0])

    def hidden_of(start, width):
        h = lax.dynamic_slice_in_dim(pre_act, start, width, 1).astype(jnp.float32)
        g = lax.dynamic_slice_in_dim(out_grad, start, width, 1).astype(jnp.float32)
        return (g * gelu_slope(h)).astype(jnp.bfloat16)

    def ring_piece(first, half):
        got = ring.swap(hidden_of(first + (1 - core) * half, half))
        mine = hidden_of(first + core * half, half)
        upper, lower = jnp.where(core == 0, mine, got), jnp.where(core == 0, got, mine)
        return jnp.concatenate([upper, lower], axis=0)

    streams, held, offsets, sent = {}, {}, {}, []
    for k, (kind, first, steps) in enumerate(chunks):
        if kind == RING:
            streams[k] = Stream(ring, ring_piece(first * STEP, steps * STEP // 2))
            half = steps // 2
            offsets[k] = jnp.stack([first + core * half, first + (1 - core) * half])
        else:
            hidden = hidden_of(first * STEP, steps * STEP)
            sent.append(hidden)
            held[k] = [lax.all_gather(hidden, "row", axis=0, tiled=True)]
            offsets[k] = jnp.full((1,), first)
        offsets[k] = offsets[k].astype(jnp.int32)
    weight_t = weight.T

    own_t = tokens.T
    x_t = jnp.zeros((rows, num_tokens), jnp.bfloat16)
    x_t = lax.dynamic_update_slice(x_t, own_t, (0, me * group))
    for s in range(1, cols):
        piece = lax.ppermute(own_t, "col", [(i, (i + s) % cols) for i in range(cols)])
        x_t = lax.dynamic_update_slice(x_t, piece, (0, (me - s) % cols * group))

    def advance(k, hops, ticks=()):
        for _ in range(hops):
            if ticks:
                streams[k].gate(list(ticks))
                ticks = ()
            streams[k].advance()

    def collect(k):
        own = merge_call(places, streams[k].pieces())
        held[k] = [own, ring.swap(own)]

    half, last = ring.hops // 2, len(chunks) - 1
    early = [k for k in streams if k < last]
    for k in early:
        advance(k, ring.hops - 1, sent)
    for k in streams:
        if k not in early:
            advance(k, half, [streams[e].fresh[0] for e in early])
    for k in early:
        advance(k, 1)
        collect(k)

    acc, outs, ticks = None, None, []
    for k in range(last):
        if k == last - 1 and last in streams:
            advance(last, ring.hops - half, ticks)
            collect(last)
            ticks = ticks + [held[last][0]]
        *outs, tick, acc = chunk_call(
            scale, offsets[k], x_t, held[k], weight_t, acc, outs, ticks, True
        )
        ticks = [tick]
    who = (me + jnp.arange(cols, dtype=jnp.int32)) % cols
    away, share = share_call(who, offsets[last], held[last], weight_t, acc, cols)
    arrived = [
        lax.ppermute(away[s - 1], "col", [(i, (i + s) % cols) for i in range(cols)])
        for s in range(1, cols)
    ]
    *outs, tick = chunk_call(
        scale, offsets[last], x_t, held[last], weight_t, None, outs, [share], False
    )
    for piece in arrived:
        share = share + piece.astype(jnp.float32)
    return (share.astype(jnp.bfloat16), *outs)


def solution(mesh):
    in_specs = (P("col", "row"), P("row", "col"), P("row", "col"), P("row", "col"))
    out_specs = (P("col", "row"), P("row", "col"), P("row", "col"), P("row", "col"))
    return jax.shard_map(
        functools.partial(on_device, mesh.shape["row"], mesh.shape["col"]),
        mesh=mesh,
        in_specs=in_specs,
        out_specs=out_specs,
        check_vma=False,
    )
```

```python
import functools
import math

import jax
import jax.numpy as jnp
import numpy as np
from jax import lax
from jax.experimental import pallas as pl
from jax.experimental.pallas import tpu as pltpu
from jax.sharding import PartitionSpec as P

BLOCK = 384
STEP = 2 * BLOCK
SHARES = (10, 6)
VMEM_LIMIT = 56 * 1024 * 1024


def gelu_slope(value):
    coeff = math.sqrt(2.0 / math.pi)
    inner = coeff * (value + 0.044715 * value * value * value)
    tanh_u = jnp.tanh(inner)
    return 0.5 * (1.0 + tanh_u) + 0.5 * value * (1.0 - tanh_u * tanh_u) * coeff * (
        1.0 + 3.0 * 0.044715 * value * value
    )


def chunk_steps(steps):
    bounds, done = [0], 0
    for share in SHARES:
        done += share
        bounds.append(round(steps * done / sum(SHARES)))
    return [(a, b - a) for a, b in zip(bounds, bounds[1:]) if b > a]


def ring_order(size):
    chips = list(range(0, size // 2, 2)) + list(range(1, size // 2, 2))[::-1]
    return [2 * chip + core for chip in chips for core in range(2)]


def add_share(acc_ref, hg_ref, w_ref):
    rows = w_ref.shape[0]
    tile = 256 if rows % 256 == 0 else rows
    for d in range(0, rows, tile):
        acc_ref[:, d : d + tile] += lax.dot_general(
            hg_ref[...],
            w_ref[d : d + tile, :],
            (((1,), (1,)), ((), ())),
            preferred_element_type=jnp.float32,
        )


def block_stats(scale, grad_f32, wg_ref, left_ref, right_ref):
    rows, cols = grad_f32.shape
    wg_ref[...] = grad_f32.astype(wg_ref.dtype)
    for i in range(rows // BLOCK):
        for j in range(cols // BLOCK):
            at = (pl.ds(i * BLOCK, BLOCK), pl.ds(j * BLOCK, BLOCK))
            tile = wg_ref[at]
            left = lax.dot_general(
                tile, tile, (((1,), (1,)), ((), ())), preferred_element_type=jnp.float32
            )
            left_ref[at] = (left * scale).astype(left_ref.dtype)
            right = lax.dot_general(
                tile, tile, (((0,), (0,)), ((), ())), preferred_element_type=jnp.float32
            )
            right_ref[at] = (right * scale).astype(right_ref.dtype)


def chunk_kernel(scale, with_share, first, *refs):
    n_in = 2 + (1 if with_share else 0) + (1 if with_share and not first else 0)
    ins, outs = refs[:n_in], refs[n_in + (0 if first else 3):]
    xt_ref, hg_ref = ins[:2]
    wg_ref, left_ref, right_ref = outs[:3]
    if with_share:
        w_ref, acc_ref = ins[2], outs[3]

        @pl.when(pl.program_id(0) == 0)
        def _():
            if first:
                acc_ref[...] = jnp.zeros_like(acc_ref)
            else:
                acc_ref[...] = ins[3][...]

        add_share(acc_ref, hg_ref, w_ref)
    grad = jnp.dot(xt_ref[...], hg_ref[...], preferred_element_type=jnp.float32)
    block_stats(scale, grad, wg_ref, left_ref, right_ref)


def chunk_call(scale, x_t, hg, weight, acc, outs, offset, steps, with_share):
    rows, tokens = x_t.shape
    first = outs is None
    at = lambda s: (0, s + offset)
    args = [x_t, hg]
    in_specs = [
        pl.BlockSpec((rows, tokens), lambda s: (0, 0)),
        pl.BlockSpec((tokens, STEP), lambda s: (0, s)),
    ]
    out_shape = [jax.ShapeDtypeStruct(weight.shape, jnp.bfloat16)] * 3
    out_specs = [pl.BlockSpec((rows, STEP), at)] * 3
    if with_share:
        args.append(weight)
        in_specs.append(pl.BlockSpec((rows, STEP), at))
        out_shape = out_shape + [jax.ShapeDtypeStruct((tokens, rows), jnp.float32)]
        out_specs = out_specs + [pl.BlockSpec((tokens, rows), lambda s: (0, 0))]
        if not first:
            args.append(acc)
            in_specs.append(pl.BlockSpec((tokens, rows), lambda s: (0, 0)))
    aliases = {}
    if not first:
        aliases = {len(args) + i: i for i in range(3)}
        args += list(outs)
        in_specs += [pl.BlockSpec(memory_space=pl.ANY)] * 3
    cells = steps * STEP * rows
    return pl.pallas_call(
        functools.partial(chunk_kernel, scale, with_share, first),
        grid=(steps,),
        in_specs=in_specs,
        out_specs=out_specs,
        out_shape=out_shape,
        input_output_aliases=aliases,
        compiler_params=pltpu.CompilerParams(vmem_limit_bytes=VMEM_LIMIT),
        cost_estimate=pl.CostEstimate(
            flops=cells * (2 * tokens * (2 if with_share else 1) + 4 * BLOCK),
            bytes_accessed=8 * cells + 2 * steps * STEP * tokens,
            transcendentals=0,
        ),
        name="chunk",
    )(*args)


def share_kernel(groups, group, each, steps, from_ref, hg_ref, w_ref, acc_ref, away_ref, own_ref, sum_ref):
    step = pl.program_id(0)

    @pl.when(step == 0)
    def _():
        sum_ref[...] = acc_ref[...]

    add_share(sum_ref, hg_ref, w_ref)

    @pl.when(step == steps - 1)
    def _():
        for k in range(groups):
            for j in range(group // each):
                at = pl.multiple_of(from_ref[k * (group // each) + j], each)
                part = sum_ref[pl.ds(at, each), :]
                to = pl.ds(j * each, each)
                if k:
                    away_ref[k - 1, to, :] = part.astype(away_ref.dtype)
                else:
                    own_ref[to, :] = part


def share_call(source, hg, weight, acc, groups, offset, steps):
    tokens, rows = acc.shape
    group = tokens // groups
    return pl.pallas_call(
        functools.partial(
            share_kernel, groups, group, tokens // source.shape[0], steps
        ),
        grid_spec=pltpu.PrefetchScalarGridSpec(
            num_scalar_prefetch=1,
            grid=(steps,),
            in_specs=[
                pl.BlockSpec((tokens, STEP), lambda s, _: (0, s)),
                pl.BlockSpec((rows, STEP), lambda s, _: (0, s + offset)),
                pl.BlockSpec((tokens, rows), lambda s, _: (0, 0)),
            ],
            out_specs=[
                pl.BlockSpec((groups - 1, group, rows), lambda s, _: (0, 0, 0)),
                pl.BlockSpec((group, rows), lambda s, _: (0, 0)),
            ],
            scratch_shapes=[pltpu.VMEM((tokens, rows), jnp.float32)],
        ),
        out_shape=[
            jax.ShapeDtypeStruct((groups - 1, group, rows), jnp.bfloat16),
            jax.ShapeDtypeStruct((group, rows), jnp.float32),
        ],
        compiler_params=pltpu.CompilerParams(vmem_limit_bytes=VMEM_LIMIT),
        cost_estimate=pl.CostEstimate(
            flops=2 * tokens * steps * STEP * rows,
            bytes_accessed=2 * steps * STEP * (rows + tokens) + 8 * tokens * rows,
            transcendentals=0,
        ),
        name="share",
    )(source, hg, weight, acc)


def on_device(row_size, cols, tokens, weight, pre_act, out_grad):
    me = lax.axis_index("col")
    group, rows = tokens.shape
    num_tokens = group * cols
    scale = 1.0 / (BLOCK * num_tokens)
    chunks = chunk_steps(weight.shape[1] // STEP)

    order, each = ring_order(row_size), pre_act.shape[0]

    gathered = []
    for offset, steps in chunks:
        at = slice(offset * STEP, (offset + steps) * STEP)
        slope = gelu_slope(pre_act[:, at].astype(jnp.float32))
        hidden = (out_grad[:, at].astype(jnp.float32) * slope).astype(jnp.bfloat16)
        gathered.append(
            lax.all_gather(hidden, "row", axis=0, tiled=True, axis_index_groups=[order])
        )

    x_all = jnp.zeros((num_tokens, rows), jnp.bfloat16)
    x_all = lax.dynamic_update_slice(x_all, tokens, (me * group, 0))
    for s in range(1, cols):
        piece = lax.ppermute(tokens, "col", [(i, (i + s) % cols) for i in range(cols)])
        x_all = lax.dynamic_update_slice(x_all, piece, ((me - s) % cols * group, 0))
    x_t = jnp.concatenate([x_all[r * each : (r + 1) * each] for r in order], axis=0).T

    acc, outs = None, None
    for (offset, steps), hg in zip(chunks[:-1], gathered[:-1]):
        *outs, acc = chunk_call(scale, x_t, hg, weight, acc, outs, offset, steps, True)

    offset, steps = chunks[-1]
    hg = gathered[-1]
    places = np.argsort(np.array(order)).astype(np.int32).reshape(cols, row_size // cols) * each
    source = jnp.asarray(places)[(me + jnp.arange(cols)) % cols].reshape(-1)
    shares, own = share_call(source, hg, weight, acc, cols, offset, steps)
    arrived = [
        lax.ppermute(shares[s - 1], "col", [(i, (i + s) % cols) for i in range(cols)])
        for s in range(1, cols)
    ]
    outs = chunk_call(scale, x_t, hg, weight, None, outs, offset, steps, False)
    for piece in arrived:
        own = own + piece.astype(jnp.float32)
    return (own.astype(jnp.bfloat16), *outs)


def solution(mesh):
    in_specs = (P("col", "row"), P("row", "col"), P("row", "col"), P("row", "col"))
    out_specs = (P("col", "row"), P("row", "col"), P("row", "col"), P("row", "col"))
    return jax.shard_map(
        functools.partial(on_device, mesh.shape["row"], mesh.shape["col"]),
        mesh=mesh,
        in_specs=in_specs,
        out_specs=out_specs,
        check_vma=False,
    )
```

```python
import functools
import math

import jax
import jax.numpy as jnp
from jax import lax
from jax.experimental import pallas as pl
from jax.experimental.pallas import tpu as pltpu
from jax.sharding import PartitionSpec as P

BLOCK = 384
STEP = 2 * BLOCK
SHARES = (11, 5)
VMEM_LIMIT = 56 * 1024 * 1024


def gelu_slope(value):
    coeff = math.sqrt(2.0 / math.pi)
    inner = coeff * (value + 0.044715 * value * value * value)
    tanh_u = jnp.tanh(inner)
    return 0.5 * (1.0 + tanh_u) + 0.5 * value * (1.0 - tanh_u * tanh_u) * coeff * (
        1.0 + 3.0 * 0.044715 * value * value
    )


def chunk_steps(steps):
    bounds, done = [0], 0
    for share in SHARES:
        done += share
        bounds.append(round(steps * done / sum(SHARES)))
    return [(a, b - a) for a, b in zip(bounds, bounds[1:]) if b > a]


def gather_order(size):
    return [2, 3, 0, 1] + list(range(4, size))


def in_order(ref, base, group, index, each):
    turn = jnp.where(index == 0, 2 * each, 0)
    parts = [
        ref[pl.ds(pl.multiple_of(base + turn, each), 2 * each), :],
        ref[pl.ds(pl.multiple_of(base + 2 * each - turn, each), 2 * each), :],
    ]
    if group > 4 * each:
        parts.append(ref[pl.ds(pl.multiple_of(base + 4 * each, each), group - 4 * each), :])
    return jnp.concatenate(parts, axis=0)


def add_share(acc_ref, hg, w_ref):
    rows = w_ref.shape[0]
    tile = 256 if rows % 256 == 0 else rows
    for d in range(0, rows, tile):
        acc_ref[:, d : d + tile] += lax.dot_general(
            hg,
            w_ref[d : d + tile, :],
            (((1,), (1,)), ((), ())),
            preferred_element_type=jnp.float32,
        )


def block_stats(scale, grad_f32, wg_ref, left_ref, right_ref):
    rows, cols = grad_f32.shape
    wg_ref[...] = grad_f32.astype(wg_ref.dtype)
    for i in range(rows // BLOCK):
        for j in range(cols // BLOCK):
            at = (pl.ds(i * BLOCK, BLOCK), pl.ds(j * BLOCK, BLOCK))
            tile = wg_ref[at]
            left = lax.dot_general(
                tile, tile, (((1,), (1,)), ((), ())), preferred_element_type=jnp.float32
            )
            left_ref[at] = (left * scale).astype(left_ref.dtype)
            right = lax.dot_general(
                tile, tile, (((0,), (0,)), ((), ())), preferred_element_type=jnp.float32
            )
            right_ref[at] = (right * scale).astype(right_ref.dtype)


def chunk_kernel(scale, each, own_only, first, who_ref, *refs):
    refs = list(refs)
    xt_ref, hg_ref, w_ref = refs[:3]
    acc_in = None if first else refs[3]
    wg_ref, left_ref, right_ref, acc_ref = refs[-4:]

    group = acc_ref.shape[0]

    @pl.when(pl.program_id(0) == 0)
    def _():
        if first:
            acc_ref[...] = jnp.zeros_like(acc_ref)
        elif own_only:
            acc_ref[...] = in_order(acc_in, 0, group, who_ref[0], each)
        else:
            acc_ref[...] = acc_in[...]

    grad = jnp.dot(xt_ref[...], hg_ref[...], preferred_element_type=jnp.float32)
    if own_only:
        me = who_ref[0]
        add_share(acc_ref, in_order(hg_ref, me * group, group, me, each), w_ref)
    else:
        add_share(acc_ref, hg_ref[...], w_ref)
    block_stats(scale, grad, wg_ref, left_ref, right_ref)


def chunk_call(scale, each, who, x_t, hg, weight, acc, outs, offset, steps, own_only):
    rows, tokens = x_t.shape
    first = outs is None
    kept = tokens // who.shape[0] if own_only else tokens
    at = lambda s, who: (0, s + offset)
    args = [x_t, hg, weight]
    in_specs = [
        pl.BlockSpec((rows, tokens), lambda s, who: (0, 0)),
        pl.BlockSpec((tokens, STEP), lambda s, who: (0, s)),
        pl.BlockSpec((rows, STEP), at),
    ]
    aliases = {}
    if not first:
        place = (lambda s, who: (who[0], 0)) if own_only else (lambda s, who: (0, 0))
        args.append(acc)
        in_specs.append(pl.BlockSpec((kept, rows), place))
        aliases = {1 + len(args) + i: i for i in range(3)}
        args += list(outs)
        in_specs += [pl.BlockSpec(memory_space=pl.ANY)] * 3
    cells = steps * STEP * rows
    return pl.pallas_call(
        functools.partial(chunk_kernel, scale, each, own_only, first),
        grid_spec=pltpu.PrefetchScalarGridSpec(
            num_scalar_prefetch=1,
            grid=(steps,),
            in_specs=in_specs,
            out_specs=[pl.BlockSpec((rows, STEP), at)] * 3
            + [pl.BlockSpec((kept, rows), lambda s, who: (0, 0))],
        ),
        out_shape=[jax.ShapeDtypeStruct(weight.shape, jnp.bfloat16)] * 3
        + [jax.ShapeDtypeStruct((kept, rows), jnp.float32)],
        input_output_aliases=aliases,
        compiler_params=pltpu.CompilerParams(vmem_limit_bytes=VMEM_LIMIT),
        cost_estimate=pl.CostEstimate(
            flops=cells * (2 * tokens + 2 * kept + 4 * BLOCK),
            bytes_accessed=8 * cells + 2 * steps * STEP * tokens,
            transcendentals=0,
        ),
        name="chunk",
    )(who, *args)


def away_kernel(each, steps, who_ref, hg_ref, w_ref, acc_ref, out_ref, sum_ref):
    step = pl.program_id(1)

    @pl.when(step == 0)
    def _():
        sum_ref[...] = acc_ref[...]

    add_share(sum_ref, hg_ref[...], w_ref)

    @pl.when(step == steps - 1)
    def _():
        index = who_ref[pl.program_id(0) + 1]
        total = in_order(sum_ref, 0, sum_ref.shape[0], index, each)
        out_ref[0] = total.astype(out_ref.dtype)


def away_call(each, who, hg, weight, acc, offset, steps):
    tokens, rows = acc.shape
    others = who.shape[0] - 1
    group = tokens // (others + 1)
    return pl.pallas_call(
        functools.partial(away_kernel, each, steps),
        grid_spec=pltpu.PrefetchScalarGridSpec(
            num_scalar_prefetch=1,
            grid=(others, steps),
            in_specs=[
                pl.BlockSpec((group, STEP), lambda p, s, who: (who[p + 1], s)),
                pl.BlockSpec((rows, STEP), lambda p, s, who: (0, s + offset)),
                pl.BlockSpec((group, rows), lambda p, s, who: (who[p + 1], 0)),
            ],
            out_specs=pl.BlockSpec((1, group, rows), lambda p, s, who: (p, 0, 0)),
            scratch_shapes=[pltpu.VMEM((group, rows), jnp.float32)],
        ),
        out_shape=jax.ShapeDtypeStruct((others, group, rows), jnp.bfloat16),
        compiler_params=pltpu.CompilerParams(vmem_limit_bytes=VMEM_LIMIT),
        cost_estimate=pl.CostEstimate(
            flops=2 * others * group * steps * STEP * rows,
            bytes_accessed=2 * steps * STEP * (rows + group) + 8 * group * rows,
            transcendentals=0,
        ),
        name="away",
    )(who, hg, weight, acc)


def on_device(row_size, cols, tokens, weight, pre_act, out_grad):
    me = lax.axis_index("col")
    group, rows = tokens.shape
    num_tokens = group * cols
    scale = 1.0 / (BLOCK * num_tokens)
    chunks = chunk_steps(weight.shape[1] // STEP)

    order, each = gather_order(row_size), pre_act.shape[0]

    gathered = []
    for offset, steps in chunks:
        at = slice(offset * STEP, (offset + steps) * STEP)
        slope = gelu_slope(pre_act[:, at].astype(jnp.float32))
        hidden = (out_grad[:, at].astype(jnp.float32) * slope).astype(jnp.bfloat16)
        gathered.append(
            lax.all_gather(hidden, "row", axis=0, tiled=True, axis_index_groups=[order])
        )

    x_all = jnp.zeros((num_tokens, rows), jnp.bfloat16)
    x_all = lax.dynamic_update_slice(x_all, tokens, (me * group, 0))
    for s in range(1, cols):
        piece = lax.ppermute(tokens, "col", [(i, (i + s) % cols) for i in range(cols)])
        x_all = lax.dynamic_update_slice(x_all, piece, ((me - s) % cols * group, 0))
    x_t = jnp.concatenate([x_all[r * each : (r + 1) * each] for r in order], axis=0).T

    who = ((me + jnp.arange(cols)) % cols).astype(jnp.int32)
    acc, outs = None, None
    for (offset, steps), hg in zip(chunks[:-1], gathered[:-1]):
        *outs, acc = chunk_call(scale, each, who, x_t, hg, weight, acc, outs, offset, steps, False)

    (offset, steps), hg = chunks[-1], gathered[-1]
    shares = away_call(each, who, hg, weight, acc, offset, steps)
    arrived = [
        lax.ppermute(shares[s - 1], "col", [(i, (i + s) % cols) for i in range(cols)])
        for s in range(1, cols)
    ]
    *outs, own = chunk_call(scale, each, who, x_t, hg, weight, acc, outs, offset, steps, True)
    for piece in arrived:
        own = own + piece.astype(jnp.float32)
    return (own.astype(jnp.bfloat16), *outs)


def solution(mesh):
    in_specs = (P("col", "row"), P("row", "col"), P("row", "col"), P("row", "col"))
    out_specs = (P("col", "row"), P("row", "col"), P("row", "col"), P("row", "col"))
    return jax.shard_map(
        functools.partial(on_device, mesh.shape["row"], mesh.shape["col"]),
        mesh=mesh,
        in_specs=in_specs,
        out_specs=out_specs,
        check_vma=False,
    )
```

```python
import functools
import math

import jax
import jax.numpy as jnp
from jax import lax
from jax.experimental import pallas as pl
from jax.experimental.pallas import tpu as pltpu
from jax.sharding import PartitionSpec as P

BLOCK = 384
STEP = 2 * BLOCK
SHARES = (11, 5)
VMEM_LIMIT = 56 * 1024 * 1024


def gelu_slope(value):
    coeff = math.sqrt(2.0 / math.pi)
    inner = coeff * (value + 0.044715 * value * value * value)
    tanh_u = jnp.tanh(inner)
    return 0.5 * (1.0 + tanh_u) + 0.5 * value * (1.0 - tanh_u * tanh_u) * coeff * (
        1.0 + 3.0 * 0.044715 * value * value
    )


def chunk_steps(steps):
    bounds, done = [0], 0
    for share in SHARES:
        done += share
        bounds.append(round(steps * done / sum(SHARES)))
    return [(a, b - a) for a, b in zip(bounds, bounds[1:]) if b > a]


def gather_order(size):
    return [2, 3, 0, 1] + list(range(4, size))


def in_order(ref, base, group, index, each):
    turn = jnp.where(index == 0, 2 * each, 0)
    parts = [
        ref[pl.ds(pl.multiple_of(base + turn, each), 2 * each), :],
        ref[pl.ds(pl.multiple_of(base + 2 * each - turn, each), 2 * each), :],
    ]
    if group > 4 * each:
        parts.append(ref[pl.ds(pl.multiple_of(base + 4 * each, each), group - 4 * each), :])
    return jnp.concatenate(parts, axis=0)


def add_share(acc_ref, hg, w_ref):
    rows = w_ref.shape[0]
    tile = 256 if rows % 256 == 0 else rows
    for d in range(0, rows, tile):
        acc_ref[:, d : d + tile] += lax.dot_general(
            hg,
            w_ref[d : d + tile, :],
            (((1,), (1,)), ((), ())),
            preferred_element_type=jnp.float32,
        )


def block_stats(scale, grad_f32, wg_ref, left_ref, right_ref):
    rows, cols = grad_f32.shape
    wg_ref[...] = grad_f32.astype(wg_ref.dtype)
    for i in range(rows // BLOCK):
        for j in range(cols // BLOCK):
            at = (pl.ds(i * BLOCK, BLOCK), pl.ds(j * BLOCK, BLOCK))
            tile = wg_ref[at]
            left = lax.dot_general(
                tile, tile, (((1,), (1,)), ((), ())), preferred_element_type=jnp.float32
            )
            left_ref[at] = (left * scale).astype(left_ref.dtype)
            right = lax.dot_general(
                tile, tile, (((0,), (0,)), ((), ())), preferred_element_type=jnp.float32
            )
            right_ref[at] = (right * scale).astype(right_ref.dtype)


def chunk_kernel(scale, with_share, first, *refs):
    refs = list(refs)
    xt_ref, hg_ref = refs[:2]
    if with_share:
        w_ref, acc_ref = refs[2], refs.pop()

        @pl.when(pl.program_id(0) == 0)
        def _():
            acc_ref[...] = jnp.zeros_like(acc_ref) if first else refs[3][...]

    grad = jnp.dot(xt_ref[...], hg_ref[...], preferred_element_type=jnp.float32)
    if with_share:
        add_share(acc_ref, hg_ref[...], w_ref)
    block_stats(scale, grad, *refs[-3:])


def chunk_call(scale, x_t, hg, weight, acc, outs, offset, steps, with_share):
    rows, tokens = x_t.shape
    first = outs is None
    at = lambda s: (0, s + offset)
    whole = pl.BlockSpec((tokens, rows), lambda s: (0, 0))
    args = [x_t, hg]
    in_specs = [
        pl.BlockSpec((rows, tokens), lambda s: (0, 0)),
        pl.BlockSpec((tokens, STEP), lambda s: (0, s)),
    ]
    out_shape = [jax.ShapeDtypeStruct(weight.shape, jnp.bfloat16)] * 3
    out_specs = [pl.BlockSpec((rows, STEP), at)] * 3
    if with_share:
        args.append(weight)
        in_specs.append(pl.BlockSpec((rows, STEP), at))
        out_shape.append(jax.ShapeDtypeStruct((tokens, rows), jnp.float32))
        out_specs.append(whole)
        if not first:
            args.append(acc)
            in_specs.append(whole)
    aliases = {}
    if not first:
        aliases = {len(args) + i: i for i in range(3)}
        args += list(outs)
        in_specs += [pl.BlockSpec(memory_space=pl.ANY)] * 3
    cells = steps * STEP * rows
    return pl.pallas_call(
        functools.partial(chunk_kernel, scale, with_share, first),
        grid=(steps,),
        in_specs=in_specs,
        out_specs=out_specs,
        out_shape=out_shape,
        input_output_aliases=aliases,
        compiler_params=pltpu.CompilerParams(vmem_limit_bytes=VMEM_LIMIT),
        cost_estimate=pl.CostEstimate(
            flops=cells * (2 * tokens * (2 if with_share else 1) + 4 * BLOCK),
            bytes_accessed=8 * cells + 2 * steps * STEP * tokens,
            transcendentals=0,
        ),
        name="chunk",
    )(*args)


def share_kernel(each, who_ref, hg_ref, w_ref, acc_ref, away_ref, own_ref, sum_ref):
    sum_ref[...] = acc_ref[...] + lax.dot_general(
        hg_ref[...], w_ref[...], (((1,), (1,)), ((), ())), preferred_element_type=jnp.float32
    )
    group = own_ref.shape[0]
    for k in range(away_ref.shape[0] + 1):
        index = who_ref[k]
        part = in_order(sum_ref, index * group, group, index, each)
        if k:
            away_ref[k - 1] = part.astype(away_ref.dtype)
        else:
            own_ref[...] = part


def share_call(each, who, hg, w_last, acc):
    tokens, rows = acc.shape
    width = hg.shape[1]
    groups = who.shape[0]
    group = tokens // groups
    tile = 256 if rows % 256 == 0 else rows
    return pl.pallas_call(
        functools.partial(share_kernel, each),
        grid_spec=pltpu.PrefetchScalarGridSpec(
            num_scalar_prefetch=1,
            grid=(rows // tile,),
            in_specs=[
                pl.BlockSpec((tokens, width), lambda d, who: (0, 0)),
                pl.BlockSpec((tile, width), lambda d, who: (d, 0)),
                pl.BlockSpec((tokens, tile), lambda d, who: (0, d)),
            ],
            out_specs=[
                pl.BlockSpec((groups - 1, group, tile), lambda d, who: (0, 0, d)),
                pl.BlockSpec((group, tile), lambda d, who: (0, d)),
            ],
            scratch_shapes=[pltpu.VMEM((tokens, tile), jnp.float32)],
        ),
        out_shape=[
            jax.ShapeDtypeStruct((groups - 1, group, rows), jnp.bfloat16),
            jax.ShapeDtypeStruct((group, rows), jnp.float32),
        ],
        compiler_params=pltpu.CompilerParams(vmem_limit_bytes=VMEM_LIMIT),
        cost_estimate=pl.CostEstimate(
            flops=2 * tokens * width * rows,
            bytes_accessed=2 * width * (rows + tokens) + 8 * tokens * rows,
            transcendentals=0,
        ),
        name="share",
    )(who, hg, w_last, acc)


def on_device(row_size, cols, tokens, weight, pre_act, out_grad):
    me = lax.axis_index("col")
    group, rows = tokens.shape
    num_tokens = group * cols
    scale = 1.0 / (BLOCK * num_tokens)
    chunks = chunk_steps(weight.shape[1] // STEP)

    order, each = gather_order(row_size), pre_act.shape[0]

    gathered = []
    for offset, steps in chunks:
        at = slice(offset * STEP, (offset + steps) * STEP)
        slope = gelu_slope(pre_act[:, at].astype(jnp.float32))
        hidden = (out_grad[:, at].astype(jnp.float32) * slope).astype(jnp.bfloat16)
        gathered.append(
            lax.all_gather(hidden, "row", axis=0, tiled=True, axis_index_groups=[order])
        )

    x_all = jnp.zeros((num_tokens, rows), jnp.bfloat16)
    x_all = lax.dynamic_update_slice(x_all, tokens, (me * group, 0))
    for s in range(1, cols):
        piece = lax.ppermute(tokens, "col", [(i, (i + s) % cols) for i in range(cols)])
        x_all = lax.dynamic_update_slice(x_all, piece, ((me - s) % cols * group, 0))
    x_t = jnp.concatenate([x_all[r * each : (r + 1) * each] for r in order], axis=0).T

    who = ((me + jnp.arange(cols)) % cols).astype(jnp.int32)
    acc, outs = None, None
    w_last = weight[:, chunks[-1][0] * STEP :]
    for (offset, steps), hg in zip(chunks[:-1], gathered[:-1]):
        *outs, acc = chunk_call(scale, x_t, hg, weight, acc, outs, offset, steps, True)

    (offset, steps), hg = chunks[-1], gathered[-1]
    shares, own = share_call(each, who, hg, w_last, acc)
    arrived = [
        lax.ppermute(shares[s - 1], "col", [(i, (i + s) % cols) for i in range(cols)])
        for s in range(1, cols)
    ]
    outs = chunk_call(scale, x_t, hg, weight, None, outs, offset, steps, False)
    for piece in arrived:
        own = own + piece.astype(jnp.float32)
    return (own.astype(jnp.bfloat16), *outs)


def solution(mesh):
    in_specs = (P("col", "row"), P("row", "col"), P("row", "col"), P("row", "col"))
    out_specs = (P("col", "row"), P("row", "col"), P("row", "col"), P("row", "col"))
    return jax.shard_map(
        functools.partial(on_device, mesh.shape["row"], mesh.shape["col"]),
        mesh=mesh,
        in_specs=in_specs,
        out_specs=out_specs,
        check_vma=False,
    )
```

```python
import functools
import math

import jax
import jax.numpy as jnp
from jax import lax
from jax.experimental import pallas as pl
from jax.experimental.pallas import tpu as pltpu
from jax.sharding import PartitionSpec as P

BLOCK = 384
STEP = 2 * BLOCK
SHARES = (11, 5)
VMEM_LIMIT = 36 * 1024 * 1024


def gelu_slope(value):
    coeff = math.sqrt(2.0 / math.pi)
    inner = coeff * (value + 0.044715 * value * value * value)
    tanh_u = jnp.tanh(inner)
    return 0.5 * (1.0 + tanh_u) + 0.5 * value * (1.0 - tanh_u * tanh_u) * coeff * (
        1.0 + 3.0 * 0.044715 * value * value
    )


def chunk_steps(steps):
    bounds, done = [0], 0
    for share in SHARES:
        done += share
        bounds.append(round(steps * done / sum(SHARES)))
    return [(a, b - a) for a, b in zip(bounds, bounds[1:]) if b > a]


def gather_order(size):
    return [2, 3, 0, 1] + list(range(4, size))


def in_order(ref, base, group, index, each):
    turn = jnp.where(index == 0, 2 * each, 0)
    parts = [
        ref[pl.ds(pl.multiple_of(base + turn, each), 2 * each), :],
        ref[pl.ds(pl.multiple_of(base + 2 * each - turn, each), 2 * each), :],
    ]
    if group > 4 * each:
        parts.append(ref[pl.ds(pl.multiple_of(base + 4 * each, each), group - 4 * each), :])
    return jnp.concatenate(parts, axis=0)


def add_share(acc_ref, hg, w_ref):
    rows = w_ref.shape[0]
    tile = 256 if rows % 256 == 0 else rows
    for d in range(0, rows, tile):
        acc_ref[:, d : d + tile] += lax.dot_general(
            hg,
            w_ref[d : d + tile, :],
            (((1,), (1,)), ((), ())),
            preferred_element_type=jnp.float32,
        )


def block_stats(scale, grad_f32, wg_ref, left_ref, right_ref):
    rows, cols = grad_f32.shape
    wg_ref[...] = grad_f32.astype(wg_ref.dtype)
    for i in range(rows // BLOCK):
        for j in range(cols // BLOCK):
            at = (pl.ds(i * BLOCK, BLOCK), pl.ds(j * BLOCK, BLOCK))
            tile = wg_ref[at]
            left = lax.dot_general(
                tile, tile, (((1,), (1,)), ((), ())), preferred_element_type=jnp.float32
            )
            left_ref[at] = (left * scale).astype(left_ref.dtype)
            right = lax.dot_general(
                tile, tile, (((0,), (0,)), ((), ())), preferred_element_type=jnp.float32
            )
            right_ref[at] = (right * scale).astype(right_ref.dtype)


def chunk_kernel(scale, with_share, first, *refs):
    refs = list(refs)
    xt_ref, hg_ref = refs[:2]
    if with_share:
        w_ref, acc_ref = refs[2], refs.pop()

        @pl.when(pl.program_id(0) == 0)
        def _():
            acc_ref[...] = jnp.zeros_like(acc_ref) if first else refs[3][...]

    grad = jnp.dot(xt_ref[...], hg_ref[...], preferred_element_type=jnp.float32)
    if with_share:
        add_share(acc_ref, hg_ref[...], w_ref)
    block_stats(scale, grad, *refs[-3:])


def chunk_call(scale, x_t, hg, weight, acc, outs, offset, steps, with_share):
    rows, tokens = x_t.shape
    first = outs is None
    at = lambda s: (0, s + offset)
    whole = pl.BlockSpec((tokens, rows), lambda s: (0, 0))
    args = [x_t, hg]
    in_specs = [
        pl.BlockSpec((rows, tokens), lambda s: (0, 0)),
        pl.BlockSpec((tokens, STEP), lambda s: (0, s)),
    ]
    out_shape = [jax.ShapeDtypeStruct(weight.shape, jnp.bfloat16)] * 3
    out_specs = [pl.BlockSpec((rows, STEP), at)] * 3
    if with_share:
        args.append(weight)
        in_specs.append(pl.BlockSpec((rows, STEP), at))
        out_shape.append(jax.ShapeDtypeStruct((tokens, rows), jnp.float32))
        out_specs.append(whole)
        if not first:
            args.append(acc)
            in_specs.append(whole)
    aliases = {}
    if not first:
        aliases = {len(args) + i: i for i in range(3)}
        args += list(outs)
        in_specs += [pl.BlockSpec(memory_space=pl.ANY)] * 3
    cells = steps * STEP * rows
    return pl.pallas_call(
        functools.partial(chunk_kernel, scale, with_share, first),
        grid=(steps,),
        in_specs=in_specs,
        out_specs=out_specs,
        out_shape=out_shape,
        input_output_aliases=aliases,
        compiler_params=pltpu.CompilerParams(vmem_limit_bytes=VMEM_LIMIT),
        cost_estimate=pl.CostEstimate(
            flops=cells * (2 * tokens * (2 if with_share else 1) + 4 * BLOCK),
            bytes_accessed=8 * cells + 2 * steps * STEP * tokens,
            transcendentals=0,
        ),
        name="chunk",
    )(*args)


def share_kernel(each, who_ref, hg_ref, w_ref, acc_ref, away_ref, own_ref, sum_ref):
    sum_ref[...] = acc_ref[...] + lax.dot_general(
        hg_ref[...], w_ref[...], (((1,), (1,)), ((), ())), preferred_element_type=jnp.float32
    )
    group = own_ref.shape[0]
    for k in range(away_ref.shape[0] + 1):
        index = who_ref[k]
        part = in_order(sum_ref, index * group, group, index, each)
        if k:
            away_ref[k - 1] = part.astype(away_ref.dtype)
        else:
            own_ref[...] = part


def share_call(each, who, hg, w_last, acc):
    tokens, rows = acc.shape
    width = hg.shape[1]
    groups = who.shape[0]
    group = tokens // groups
    tile = 256 if rows % 256 == 0 else rows
    return pl.pallas_call(
        functools.partial(share_kernel, each),
        grid_spec=pltpu.PrefetchScalarGridSpec(
            num_scalar_prefetch=1,
            grid=(rows // tile,),
            in_specs=[
                pl.BlockSpec((tokens, width), lambda d, who: (0, 0)),
                pl.BlockSpec((tile, width), lambda d, who: (d, 0)),
                pl.BlockSpec((tokens, tile), lambda d, who: (0, d)),
            ],
            out_specs=[
                pl.BlockSpec((groups - 1, group, tile), lambda d, who: (0, 0, d)),
                pl.BlockSpec((group, tile), lambda d, who: (0, d)),
            ],
            scratch_shapes=[pltpu.VMEM((tokens, tile), jnp.float32)],
        ),
        out_shape=[
            jax.ShapeDtypeStruct((groups - 1, group, rows), jnp.bfloat16),
            jax.ShapeDtypeStruct((group, rows), jnp.float32),
        ],
        compiler_params=pltpu.CompilerParams(vmem_limit_bytes=VMEM_LIMIT),
        cost_estimate=pl.CostEstimate(
            flops=2 * tokens * width * rows,
            bytes_accessed=2 * width * (rows + tokens) + 8 * tokens * rows,
            transcendentals=0,
        ),
        name="share",
    )(who, hg, w_last, acc)


def on_device(row_size, cols, tokens, weight, pre_act, out_grad):
    me = lax.axis_index("col")
    group, rows = tokens.shape
    num_tokens = group * cols
    scale = 1.0 / (BLOCK * num_tokens)
    chunks = chunk_steps(weight.shape[1] // STEP)

    order, each = gather_order(row_size), pre_act.shape[0]

    gathered = []
    for offset, steps in chunks:
        at = slice(offset * STEP, (offset + steps) * STEP)
        slope = gelu_slope(pre_act[:, at].astype(jnp.float32))
        hidden = (out_grad[:, at].astype(jnp.float32) * slope).astype(jnp.bfloat16)
        gathered.append(
            lax.all_gather(hidden, "row", axis=0, tiled=True, axis_index_groups=[order])
        )

    x_all = jnp.zeros((num_tokens, rows), jnp.bfloat16)
    x_all = lax.dynamic_update_slice(x_all, tokens, (me * group, 0))
    for s in range(1, cols):
        piece = lax.ppermute(tokens, "col", [(i, (i + s) % cols) for i in range(cols)])
        x_all = lax.dynamic_update_slice(x_all, piece, ((me - s) % cols * group, 0))
    x_t = jnp.concatenate([x_all[r * each : (r + 1) * each] for r in order], axis=0).T

    who = ((me + jnp.arange(cols)) % cols).astype(jnp.int32)
    acc, outs = None, None
    w_last = weight[:, chunks[-1][0] * STEP :]
    for (offset, steps), hg in zip(chunks[:-1], gathered[:-1]):
        *outs, acc = chunk_call(scale, x_t, hg, weight, acc, outs, offset, steps, True)

    (offset, steps), hg = chunks[-1], gathered[-1]
    shares, own = share_call(each, who, hg, w_last, acc)
    arrived = [
        lax.ppermute(shares[s - 1], "col", [(i, (i + s) % cols) for i in range(cols)])
        for s in range(1, cols)
    ]
    outs = chunk_call(scale, x_t, hg, weight, None, outs, offset, steps, False)
    for piece in arrived:
        own = own + piece.astype(jnp.float32)
    return (own.astype(jnp.bfloat16), *outs)


def solution(mesh):
    in_specs = (P("col", "row"), P("row", "col"), P("row", "col"), P("row", "col"))
    out_specs = (P("col", "row"), P("row", "col"), P("row", "col"), P("row", "col"))
    return jax.shard_map(
        functools.partial(on_device, mesh.shape["row"], mesh.shape["col"]),
        mesh=mesh,
        in_specs=in_specs,
        out_specs=out_specs,
        check_vma=False,
    )
```

```python
import functools
import math

import jax
import jax.numpy as jnp
from jax import lax
from jax.experimental import pallas as pl
from jax.experimental.pallas import tpu as pltpu
from jax.sharding import PartitionSpec as P

BLOCK = 384
STEP = 2 * BLOCK
SHARES = (11, 5)
VMEM_LIMIT = 56 * 1024 * 1024


def gelu_slope(value):
    coeff = math.sqrt(2.0 / math.pi)
    square = value * value
    tanh_u = jnp.tanh(value * (coeff + (coeff * 0.044715) * square))
    slope_u = value * (coeff + (3.0 * coeff * 0.044715) * square)
    return (0.5 + 0.5 * tanh_u) * (1.0 + (1.0 - tanh_u) * slope_u)


def chunk_steps(steps):
    bounds, done = [0], 0
    for share in SHARES:
        done += share
        bounds.append(round(steps * done / sum(SHARES)))
    return [(a, b - a) for a, b in zip(bounds, bounds[1:]) if b > a]


def gather_order(size):
    return [2, 3, 0, 1] + list(range(4, size))


def in_order(ref, base, group, index, each):
    turn = jnp.where(index == 0, 2 * each, 0)
    parts = [
        ref[pl.ds(pl.multiple_of(base + turn, each), 2 * each), :],
        ref[pl.ds(pl.multiple_of(base + 2 * each - turn, each), 2 * each), :],
    ]
    if group > 4 * each:
        parts.append(ref[pl.ds(pl.multiple_of(base + 4 * each, each), group - 4 * each), :])
    return jnp.concatenate(parts, axis=0)


def add_share(acc_ref, hg, w_ref):
    rows = w_ref.shape[0]
    tile = 256 if rows % 256 == 0 else rows
    for d in range(0, rows, tile):
        acc_ref[:, d : d + tile] += lax.dot_general(
            hg,
            w_ref[d : d + tile, :],
            (((1,), (1,)), ((), ())),
            preferred_element_type=jnp.float32,
        )


def block_stats(scale, grad_f32, wg_ref, left_ref, right_ref):
    rows, cols = grad_f32.shape
    wg_ref[...] = grad_f32.astype(wg_ref.dtype)
    for i in range(rows // BLOCK):
        for j in range(cols // BLOCK):
            at = (pl.ds(i * BLOCK, BLOCK), pl.ds(j * BLOCK, BLOCK))
            tile = wg_ref[at]
            left = lax.dot_general(
                tile, tile, (((1,), (1,)), ((), ())), preferred_element_type=jnp.float32
            )
            left_ref[at] = (left * scale).astype(left_ref.dtype)
            right = lax.dot_general(
                tile, tile, (((0,), (0,)), ((), ())), preferred_element_type=jnp.float32
            )
            right_ref[at] = (right * scale).astype(right_ref.dtype)


def chunk_kernel(scale, with_share, first, *refs):
    refs = list(refs)
    xt_ref, hg_ref = refs[:2]
    if with_share:
        w_ref, acc_ref = refs[2], refs.pop()

        @pl.when(pl.program_id(0) == 0)
        def _():
            acc_ref[...] = jnp.zeros_like(acc_ref) if first else refs[3][...]

    grad = jnp.dot(xt_ref[...], hg_ref[...], preferred_element_type=jnp.float32)
    if with_share:
        add_share(acc_ref, hg_ref[...], w_ref)
    block_stats(scale, grad, *refs[-3:])


def chunk_call(scale, x_t, hg, weight, acc, outs, offset, steps, with_share):
    rows, tokens = x_t.shape
    first = outs is None
    at = lambda s: (0, s + offset)
    whole = pl.BlockSpec((tokens, rows), lambda s: (0, 0))
    args = [x_t, hg]
    in_specs = [
        pl.BlockSpec((rows, tokens), lambda s: (0, 0)),
        pl.BlockSpec((tokens, STEP), lambda s: (0, s)),
    ]
    out_shape = [jax.ShapeDtypeStruct(weight.shape, jnp.bfloat16)] * 3
    out_specs = [pl.BlockSpec((rows, STEP), at)] * 3
    if with_share:
        args.append(weight)
        in_specs.append(pl.BlockSpec((rows, STEP), at))
        out_shape.append(jax.ShapeDtypeStruct((tokens, rows), jnp.float32))
        out_specs.append(whole)
        if not first:
            args.append(acc)
            in_specs.append(whole)
    aliases = {}
    if not first:
        aliases = {len(args) + i: i for i in range(3)}
        args += list(outs)
        in_specs += [pl.BlockSpec(memory_space=pl.ANY)] * 3
    cells = steps * STEP * rows
    return pl.pallas_call(
        functools.partial(chunk_kernel, scale, with_share, first),
        grid=(steps,),
        in_specs=in_specs,
        out_specs=out_specs,
        out_shape=out_shape,
        input_output_aliases=aliases,
        compiler_params=pltpu.CompilerParams(vmem_limit_bytes=VMEM_LIMIT),
        cost_estimate=pl.CostEstimate(
            flops=cells * (2 * tokens * (2 if with_share else 1) + 4 * BLOCK),
            bytes_accessed=8 * cells + 2 * steps * STEP * tokens,
            transcendentals=0,
        ),
        name="chunk",
    )(*args)


def share_kernel(each, who_ref, hg_ref, w_ref, acc_ref, away_ref, own_ref, sum_ref):
    sum_ref[...] = acc_ref[...] + lax.dot_general(
        hg_ref[...], w_ref[...], (((1,), (1,)), ((), ())), preferred_element_type=jnp.float32
    )
    group = own_ref.shape[0]
    for k in range(away_ref.shape[0] + 1):
        index = who_ref[k]
        part = in_order(sum_ref, index * group, group, index, each)
        if k:
            away_ref[k - 1] = part.astype(away_ref.dtype)
        else:
            own_ref[...] = part


def share_call(each, who, hg, w_last, acc):
    tokens, rows = acc.shape
    width = hg.shape[1]
    groups = who.shape[0]
    group = tokens // groups
    tile = 256 if rows % 256 == 0 else rows
    return pl.pallas_call(
        functools.partial(share_kernel, each),
        grid_spec=pltpu.PrefetchScalarGridSpec(
            num_scalar_prefetch=1,
            grid=(rows // tile,),
            in_specs=[
                pl.BlockSpec((tokens, width), lambda d, who: (0, 0)),
                pl.BlockSpec((tile, width), lambda d, who: (d, 0)),
                pl.BlockSpec((tokens, tile), lambda d, who: (0, d)),
            ],
            out_specs=[
                pl.BlockSpec((groups - 1, group, tile), lambda d, who: (0, 0, d)),
                pl.BlockSpec((group, tile), lambda d, who: (0, d)),
            ],
            scratch_shapes=[pltpu.VMEM((tokens, tile), jnp.float32)],
        ),
        out_shape=[
            jax.ShapeDtypeStruct((groups - 1, group, rows), jnp.bfloat16),
            jax.ShapeDtypeStruct((group, rows), jnp.float32),
        ],
        compiler_params=pltpu.CompilerParams(vmem_limit_bytes=VMEM_LIMIT),
        cost_estimate=pl.CostEstimate(
            flops=2 * tokens * width * rows,
            bytes_accessed=2 * width * (rows + tokens) + 8 * tokens * rows,
            transcendentals=0,
        ),
        name="share",
    )(who, hg, w_last, acc)


def on_device(row_size, cols, tokens, weight, pre_act, out_grad):
    me = lax.axis_index("col")
    group, rows = tokens.shape
    num_tokens = group * cols
    scale = 1.0 / (BLOCK * num_tokens)
    chunks = chunk_steps(weight.shape[1] // STEP)

    order, each = gather_order(row_size), pre_act.shape[0]

    gathered = []
    for offset, steps in chunks:
        at = slice(offset * STEP, (offset + steps) * STEP)
        slope = gelu_slope(pre_act[:, at].astype(jnp.float32))
        hidden = (out_grad[:, at].astype(jnp.float32) * slope).astype(jnp.bfloat16)
        gathered.append(
            lax.all_gather(hidden, "row", axis=0, tiled=True, axis_index_groups=[order])
        )

    x_all = jnp.zeros((num_tokens, rows), jnp.bfloat16)
    x_all = lax.dynamic_update_slice(x_all, tokens, (me * group, 0))
    for s in range(1, cols):
        piece = lax.ppermute(tokens, "col", [(i, (i + s) % cols) for i in range(cols)])
        x_all = lax.dynamic_update_slice(x_all, piece, ((me - s) % cols * group, 0))
    x_t = jnp.concatenate([x_all[r * each : (r + 1) * each] for r in order], axis=0).T

    who = ((me + jnp.arange(cols)) % cols).astype(jnp.int32)
    acc, outs = None, None
    w_last = weight[:, chunks[-1][0] * STEP :]
    for (offset, steps), hg in zip(chunks[:-1], gathered[:-1]):
        *outs, acc = chunk_call(scale, x_t, hg, weight, acc, outs, offset, steps, True)

    (offset, steps), hg = chunks[-1], gathered[-1]
    shares, own = share_call(each, who, hg, w_last, acc)
    arrived = [
        lax.ppermute(shares[s - 1], "col", [(i, (i + s) % cols) for i in range(cols)])
        for s in range(1, cols)
    ]
    outs = chunk_call(scale, x_t, hg, weight, None, outs, offset, steps, False)
    for piece in arrived:
        own = own + piece.astype(jnp.float32)
    return (own.astype(jnp.bfloat16), *outs)


def solution(mesh):
    in_specs = (P("col", "row"), P("row", "col"), P("row", "col"), P("row", "col"))
    out_specs = (P("col", "row"), P("row", "col"), P("row", "col"), P("row", "col"))
    return jax.shard_map(
        functools.partial(on_device, mesh.shape["row"], mesh.shape["col"]),
        mesh=mesh,
        in_specs=in_specs,
        out_specs=out_specs,
        check_vma=False,
    )
```
